32 devices in a mesh: groups: 2 (over x), src: 16 (over z, y, core).
Axes of the slice: x: 2, y: 2, z: 4, core: 2. Of those that a mesh axis runs over, the one named last changes fastest.
Arguments:
- layout_mask: int32 [512, 256], P('groups'), parts along dimension 0, may hold values 0 or 1
- source_coords: int32 [32, 2], P('src'), may hold values from -8 to 8
- source_weights: int32 [32], P('src'), may hold values from 1 to 8
- focus_steps: int32 [16], replicated, may hold values from -4 to 4
- pupil_taps: float32 [48], replicated, may hold values from 0.25 to 1.75
- blur_x: float32 [31], replicated, may hold values from 0 to 2
- blur_y: float32 [31], replicated, may hold values from 0 to 2
- blur_z: float32 [31], replicated, may hold values from 0 to 2
Outputs:
- intensity: float32 [8192, 256], P(('groups', 'src')), parts along dimension 0
- latent: float32 [8192, 256], P(('groups', 'src')), parts along dimension 0
The draws below stay inside these ranges and needn't reach their ends.
There are 2 independent parts, one for each index of `groups`. The reference program is written for one: setup_inputs(seed, part) draws one part's arguments, and reference() takes and returns one part's arrays. A program takes and returns all parts, laid end to end along the dimension named above; an argument that names none is the same for every part. Nothing has to cross between parts.
All inputs are finite; a program needn't handle non-finite values.
Results may differ from the reference program's by a relative error of at most 0.0022.
Values sent between devices are 32-bit elements; how exact they have to be, the bound alone decides.
A program may use at most 64 MiB of HBM per device.

```python
import math
import jax
import jax.numpy as jnp
from jax import lax

H = 256
W = 256
F = 16
PT = 48
HB = 15
S = 32


def set_ends(drawn, rng, least, high):
    longest = drawn.shape.index(max(drawn.shape))
    spots = []
    for shift in (0, 1):
        where = [jax.random.randint(jax.random.fold_in(rng, axis), (), 0, length) for axis, length in enumerate(drawn.shape)]
        where[longest] = (where[longest] + shift) % drawn.shape[longest]
        spots.append(tuple(where))
    return drawn.at[spots[0]].set(least).at[spots[1]].set(high)


def setup_inputs(seed: int = 0, part: int = 0) -> dict:
    splits = jax.random.split(jax.random.key(seed), 9)
    part_splits = jax.random.split(jax.random.fold_in(splits[8], part), 9)
    layout_mask = set_ends((jax.random.randint(part_splits[0], (H, W), 0, 5) < 2).astype(jnp.int32), jax.random.fold_in(part_splits[0], 1), 0, 1)
    source_coords = set_ends(jax.random.randint(splits[1], (S, 2), -8, 9), jax.random.fold_in(splits[1], 1), -8, 8).astype(jnp.int32)
    source_weights = set_ends(jax.random.randint(splits[2], (S,), 1, 9), jax.random.fold_in(splits[2], 1), 1, 8).astype(jnp.int32)
    focus_steps = set_ends(jax.random.randint(splits[3], (F,), -4, 5), jax.random.fold_in(splits[3], 1), -4, 4).astype(jnp.int32)
    pupil_taps = jnp.clip(1.0 + 0.15 * jax.random.normal(splits[4], (PT,), jnp.float32), 0.25, 1.75)
    blur_x = jnp.clip(jax.random.uniform(splits[5], (2 * HB + 1,), jnp.float32, 0.0, 2.0), 0.0, 2.0)
    blur_y = jnp.clip(jax.random.uniform(splits[6], (2 * HB + 1,), jnp.float32, 0.0, 2.0), 0.0, 2.0)
    blur_z = jnp.clip(jax.random.uniform(splits[7], (2 * F - 1,), jnp.float32, 0.0, 2.0), 0.0, 2.0)
    return {"layout_mask": layout_mask, "source_coords": source_coords, "source_weights": source_weights, "focus_steps": focus_steps, "pupil_taps": pupil_taps, "blur_x": blur_x, "blur_y": blur_y, "blur_z": blur_z}


two_pi = 2.0 * math.pi
defocus_scale = 0.8
dose_scale = 2.0

def to_wide(values):
    return lax.optimization_barrier(values.astype(jnp.bfloat16)).astype(jnp.float32)

def tap_matrix(out_pos, extent, tilt_index, focus_step, pupil_taps):
    tap_count = pupil_taps.shape[0]
    centre = (tap_count - 1) / 2.0
    column_pos = jnp.arange(extent, dtype=jnp.int32)
    offset = column_pos[None, :] - out_pos[:, None] + tap_count // 2
    inside = (offset >= 0) & (offset < tap_count)
    clipped = jnp.clip(offset, 0, tap_count - 1).astype(jnp.int32)
    amplitude = jnp.take(pupil_taps, clipped) / math.sqrt(tap_count)
    relative = clipped.astype(jnp.float32) - centre
    phase_angle = two_pi * tilt_index.astype(jnp.float32) * relative / tap_count + defocus_scale * focus_step.astype(jnp.float32) * (relative / centre) ** 2
    real_part = jnp.where(inside, amplitude * jnp.cos(phase_angle), jnp.zeros_like(amplitude))
    imag_part = jnp.where(inside, amplitude * jnp.sin(phase_angle), jnp.zeros_like(amplitude))
    return (to_wide(real_part), to_wide(imag_part))

def field_power(mask_wide, tilt_x, tilt_y, focus_step, pupil_taps):
    rows_tile, cols_tile = mask_wide.shape
    row_pos = jnp.arange(rows_tile, dtype=jnp.int32)
    col_pos = jnp.arange(cols_tile, dtype=jnp.int32)
    rows_real, rows_imag = tap_matrix(row_pos, rows_tile, tilt_y, focus_step, pupil_taps)
    cols_real, cols_imag = tap_matrix(col_pos, cols_tile, tilt_x, focus_step, pupil_taps)
    stacked = jnp.concatenate([rows_real, rows_imag], axis=0)
    first_pass = to_wide(jnp.dot(stacked, mask_wide, precision=lax.Precision.HIGHEST))
    joined = jnp.concatenate([first_pass[:rows_tile], first_pass[rows_tile:]], axis=1)
    upper_half = jnp.concatenate([cols_real.T, cols_imag.T], axis=1)
    lower_half = jnp.concatenate([-cols_imag.T, cols_real.T], axis=1)
    pupil_cols = jnp.concatenate([upper_half, lower_half], axis=0)
    field_parts = jnp.dot(joined, pupil_cols, precision=lax.Precision.HIGHEST)
    return field_parts[:, :cols_tile] ** 2 + field_parts[:, cols_tile:] ** 2

def reference(layout_mask, source_coords, source_weights, focus_steps, pupil_taps, blur_x, blur_y, blur_z):
    rows_tile, cols_tile = layout_mask.shape
    planes = focus_steps.shape[0]
    total_src = source_coords.shape[0]
    mask_wide = layout_mask.astype(jnp.float32)
    factors = source_weights.astype(jnp.float32) / (4.0 * total_src)

    def add_source(running, source_item):
        point_coords, weight_factor = source_item

        def one_plane(focus_step):
            return field_power(mask_wide, point_coords[0], point_coords[1], focus_step, pupil_taps)
        powers = lax.map(one_plane, focus_steps)
        return (running + weight_factor * powers, None)
    start_stack = jnp.zeros((planes, rows_tile, cols_tile), jnp.float32)
    intensity_stack = lax.scan(add_source, start_stack, (source_coords, factors))[0]
    intensity = intensity_stack.reshape(planes * rows_tile, cols_tile)
    acid_level = 1.0 - jnp.exp(-dose_scale * intensity)
    width_x = blur_x.shape[0]
    half_x = width_x // 2
    padded = jnp.pad(acid_level, ((0, 0), (half_x, half_x)))
    along_x = jnp.zeros_like(acid_level)
    for tap_index in range(width_x):
        along_x = along_x + blur_x[tap_index] / width_x * padded[:, tap_index:tap_index + cols_tile]
    width_y = blur_y.shape[0]
    half_y = width_y // 2
    total_rows = planes * rows_tile
    padded = jnp.pad(along_x, ((half_y, half_y), (0, 0)))
    along_y = jnp.zeros_like(along_x)
    for tap_index in range(width_y):
        along_y = along_y + blur_y[tap_index] / width_y * padded[tap_index:tap_index + total_rows, :]
    along_y = along_y.reshape(planes, rows_tile, cols_tile)
    plane_pos = jnp.arange(planes, dtype=jnp.int32)
    lag_index = (plane_pos[:, None] - plane_pos[None, :] + planes - 1).astype(jnp.int32)
    focus_matrix = jnp.take(blur_z, lag_index) / planes
    latent = jnp.einsum('pq,qyx->pyx', focus_matrix, along_y, precision=lax.Precision.HIGHEST)
    return (intensity, latent.reshape(planes * rows_tile, cols_tile))
```

```python
import math

import jax
import jax.numpy as jnp
from jax import lax
from jax.experimental import pallas as pl
from jax.experimental.pallas import tpu as pltpu
from jax.sharding import PartitionSpec as P

two_pi = 2.0 * math.pi
defocus_scale = 0.8
dose_scale = 2.0


def extended_2(block, sides, width):
    for axis, dim in sides:
        count = lax.axis_size(axis)
        forward = [(i, i + 1) for i in range(count - 1)]
        backward = [(target, source) for source, target in forward]
        low = lax.ppermute(
            lax.slice_in_dim(block, block.shape[dim] - width, None, axis=dim), axis, forward
        )
        high = lax.ppermute(lax.slice_in_dim(block, 0, width, axis=dim), axis, backward)
        block = jnp.concatenate([low, block, high], axis=dim)
    return block


def passed_along(block, axis, distance):
    devices = range(lax.axis_size(axis))
    route = [(i - distance, i) for i in devices if i - distance in devices]
    return lax.ppermute(block, axis, route)


def tap_matrix(out_pos, extent, tilt_index, focus_step, pupil_taps):
    tap_count = pupil_taps.shape[0]
    centre = (tap_count - 1) / 2.0
    column_pos = jnp.arange(extent, dtype=jnp.int32)
    offset = column_pos[None, :] - out_pos[:, None] + tap_count // 2
    inside = (offset >= 0) & (offset < tap_count)
    clipped = jnp.clip(offset, 0, tap_count - 1)
    amplitude = jnp.take(pupil_taps, clipped) / math.sqrt(tap_count)
    relative = clipped.astype(jnp.float32) - centre
    phase_angle = (
        two_pi * tilt_index.astype(jnp.float32) * relative / tap_count
        + defocus_scale * focus_step.astype(jnp.float32) * (relative / centre) ** 2
    )
    real_part = jnp.where(inside, amplitude * jnp.cos(phase_angle), jnp.zeros_like(amplitude))
    imag_part = jnp.where(inside, amplitude * jnp.sin(phase_angle), jnp.zeros_like(amplitude))
    return (real_part.astype(jnp.bfloat16), imag_part.astype(jnp.bfloat16))


def field_power(mask_bf, row_pos, tilt_x, tilt_y, focus_step, pupil_taps):
    rows_tile, cols_tile = mask_bf.shape
    row_count = row_pos.shape[0]
    col_pos = jnp.arange(cols_tile, dtype=jnp.int32)
    rows_real, rows_imag = tap_matrix(row_pos, rows_tile, tilt_y, focus_step, pupil_taps)
    cols_real, cols_imag = tap_matrix(col_pos, cols_tile, tilt_x, focus_step, pupil_taps)
    stacked = jnp.concatenate([rows_real, rows_imag], axis=0)
    first_pass = jnp.dot(stacked, mask_bf, preferred_element_type=jnp.float32).astype(jnp.bfloat16)
    joined = jnp.concatenate([first_pass[:row_count], first_pass[row_count:]], axis=1)
    upper_half = jnp.concatenate([cols_real.T, cols_imag.T], axis=1)
    lower_half = jnp.concatenate([-cols_imag.T, cols_real.T], axis=1)
    pupil_cols = jnp.concatenate([upper_half, lower_half], axis=0)
    field_parts = jnp.dot(joined, pupil_cols, preferred_element_type=jnp.float32)
    return field_parts[:, :cols_tile] ** 2 + field_parts[:, cols_tile:] ** 2


def on_device(
    layout_mask, source_coords, source_weights, focus_steps, pupil_taps, blur_x, blur_y, blur_z
):
    rows_tile, cols_tile = layout_mask.shape
    planes = focus_steps.shape[0]
    devices = lax.axis_size("src")
    src_local = source_coords.shape[0]
    mask_bf = layout_mask.astype(jnp.bfloat16)
    own_rows = planes * rows_tile // devices
    per_plane = devices // planes
    factors = source_weights.astype(jnp.float32) / (4.0 * src_local * devices)
    row_pos = jnp.arange(rows_tile, dtype=jnp.int32)

    def plane_term(focus_step):
        running = jnp.zeros((rows_tile, cols_tile), jnp.float32)
        for source in range(src_local):
            power = field_power(
                mask_bf,
                row_pos,
                source_coords[source, 0],
                source_coords[source, 1],
                focus_step,
                pupil_taps,
            )
            running = running + factors[source] * power
        return running

    partial_sum = lax.map(plane_term, focus_steps).reshape(planes * rows_tile, cols_tile)
    intensity = lax.psum_scatter(partial_sum, "src", scatter_dimension=0, tiled=True)
    acid_level = 1.0 - jnp.exp(-dose_scale * intensity)
    width_x = blur_x.shape[0]
    half_x = width_x // 2
    padded = jnp.pad(acid_level, ((0, 0), (half_x, half_x)))
    along_x = jnp.zeros_like(acid_level)
    for tap_index in range(width_x):
        along_x = (
            along_x + blur_x[tap_index] / width_x * padded[:, tap_index : tap_index + cols_tile]
        )
    width_y = blur_y.shape[0]
    half_y = width_y // 2
    extended = extended_2(along_x, (("src", 0),), half_y)
    along_y = jnp.zeros_like(along_x)
    for tap_index in range(width_y):
        along_y = along_y + blur_y[tap_index] / width_y * extended[tap_index : tap_index + own_rows]
    latent = blur_z[planes - 1] / planes * along_y
    for plane_lag in range(1 - planes, planes):
        if plane_lag != 0:
            arrived = passed_along(along_y, "src", plane_lag * per_plane)
            latent = latent + blur_z[plane_lag + planes - 1] / planes * arrived
    return (intensity, latent)


max_shift = 8
shifts = 2 * max_shift + 1
lanes = 512


def exact_dot(left, right):
    return jnp.dot(left, right, precision=lax.Precision.HIGHEST, preferred_element_type=jnp.float32)


def store_toeplitz(row, position, pieces):
    base = pltpu.roll(jnp.broadcast_to(row, (16, lanes)), position, 1, stride=1, stride_axis=0)
    for j in range(8):
        rolled = pltpu.roll(base, lanes - 128 + 16 * j, 1)
        for block, start in ((j + 8, 0), (j, 128)):
            part = rolled[:, start : start + 256]
            for ref, top, side, sign in pieces:
                value = part if sign > 0 else -part
                ref[top + 16 * block : top + 16 * block + 16, side : side + 256] = value.astype(
                    ref.dtype
                )


def store_taps(taps_ref, row, focus, flip, real_ref, imag_ref, tap_count):
    centre = (tap_count - 1) / 2.0
    amplitude = taps_ref[row : row + 1, :128] / math.sqrt(tap_count)
    shape = (24, 128)
    relative = (lax.broadcasted_iota(jnp.int32, shape, 1).astype(jnp.float32) - centre) * flip
    tilt = (lax.broadcasted_iota(jnp.int32, shape, 0) - max_shift).astype(jnp.float32)
    phase = (
        two_pi * tilt * relative / tap_count + defocus_scale * focus * (relative / centre) ** 2
    )
    real_ref[...] = jnp.zeros_like(real_ref)
    imag_ref[...] = jnp.zeros_like(imag_ref)
    real_ref[:, :128] = amplitude * jnp.cos(phase)
    imag_ref[:, :128] = amplitude * jnp.sin(phase)


def build_tables(tap_count, mask_ref, rows_ref, focus, tap_refs, stacked, fields, pupils):
    forward_real, forward_imag, back_real, back_imag = tap_refs
    store_taps(rows_ref, 0, focus, 1.0, forward_real, forward_imag, tap_count)
    store_taps(rows_ref, 1, focus, -1.0, back_real, back_imag, tap_count)
    mask_bf = mask_ref[...].astype(jnp.float32).astype(jnp.bfloat16)

    def one_shift(shift, carry):
        row = pl.ds(shift, 1)
        store_toeplitz(forward_real[row, :], 232, ((stacked, 0, 0, 1),))
        store_toeplitz(forward_imag[row, :], 232, ((stacked, 256, 0, 1),))
        first = jnp.dot(stacked[...], mask_bf, preferred_element_type=jnp.float32)
        fields[shift, :, :256] = first[:256].astype(jnp.bfloat16)
        fields[shift, :, 256:] = first[256:].astype(jnp.bfloat16)
        pupil = pupils.at[shift]
        store_toeplitz(back_real[row, :], 233, ((pupil, 0, 0, 1), (pupil, 256, 256, 1)))
        store_toeplitz(back_imag[row, :], 233, ((pupil, 0, 256, 1), (pupil, 256, 0, -1)))
        return carry

    lax.fori_loop(0, shifts, one_shift, 0)


def image_kernel(
    tap_count, points_ref, focus_ref, mask_ref, rows_ref, intensity_ref, along_ref,
    t0, t1, t2, t3, stacked, fields, pupils, blur,
):
    me = lax.axis_index("src")
    total = points_ref.shape[0]
    focus = focus_ref[me].astype(jnp.float32)
    build_tables(tap_count, mask_ref, rows_ref, focus, (t0, t1, t2, t3), stacked, fields, pupils)
    store_toeplitz(rows_ref[2:3, :], 241, ((blur, 0, 0, 1),))
    intensity_ref[...] = jnp.zeros_like(intensity_ref)

    def one_source(s, carry):
        factor = points_ref[s, 2].astype(jnp.float32) / (4.0 * total)
        field = jnp.dot(
            fields[points_ref[s, 1] + max_shift],
            pupils[points_ref[s, 0] + max_shift],
            preferred_element_type=jnp.float32,
        )
        intensity_ref[...] += factor * (field[:, :256] ** 2 + field[:, 256:] ** 2)
        return carry

    lax.fori_loop(0, total, one_source, 0)
    acid = 1.0 - jnp.exp(-dose_scale * intensity_ref[...])
    along_ref[...] = exact_dot(blur[...], acid.T)


def stack_blur(stack, rows_ref, blur_z_ref, centre, planes, wide):
    back_y = rows_ref[3:4, :]
    store_toeplitz(back_y, 241, ((centre, 0, 0, 1),))
    tall = jnp.broadcast_to(back_y, (16, lanes))
    before = pltpu.roll(tall, lanes - 31, 1, stride=1, stride_axis=0)[:, :256]
    after = pltpu.roll(tall, 241, 1, stride=1, stride_axis=0)[:, :256]
    pad = jnp.zeros((240, 256), jnp.float32)
    zero = jnp.zeros((wide, 256), jnp.float32)
    along_y = (
        exact_dot(stack, centre[...])
        + exact_dot(
            jnp.concatenate([zero, stack[:-wide]], axis=0), jnp.concatenate([pad, before], axis=0)
        )
        + exact_dot(
            jnp.concatenate([stack[wide:], zero], axis=0), jnp.concatenate([after, pad], axis=0)
        )
    )
    distance = lax.broadcasted_iota(jnp.int32, (256, 256), 0) - lax.broadcasted_iota(
        jnp.int32, (256, 256), 1
    )
    mix = jnp.zeros((256, 256), jnp.float32)
    for lag in range(1 - planes, planes):
        mix = jnp.where(distance == lag * wide, blur_z_ref[lag + planes - 1] / planes, mix)
    return exact_dot(mix, along_y)


def stack_kernel(planes, wide, blur_z_ref, stack_ref, rows_ref, out_ref, centre):
    out_ref[...] = stack_blur(stack_ref[...], rows_ref, blur_z_ref, centre, planes, wide)


def padded_rows(pupil_taps, blur_x, blur_y):
    parts = (
        pupil_taps,
        pupil_taps[::-1],
        blur_x / blur_x.shape[0],
        (blur_y / blur_y.shape[0])[::-1],
    )
    rows = [jnp.pad(part, (0, lanes - part.shape[0])) for part in parts]
    return jnp.concatenate([jnp.stack(rows), jnp.zeros((4, lanes), jnp.float32)], axis=0)


vmem = pl.BlockSpec(memory_space=pltpu.VMEM)
smem = pl.BlockSpec(memory_space=pltpu.SMEM)


def table_scratch():
    return [pltpu.VMEM((24, lanes), jnp.float32)] * 4 + [
        pltpu.VMEM((512, 256), jnp.bfloat16),
        pltpu.VMEM((shifts, 256, 512), jnp.bfloat16),
        pltpu.VMEM((shifts, 512, 512), jnp.bfloat16),
        pltpu.VMEM((256, 256), jnp.float32),
    ]


def plane_per_device(
    layout_mask, source_coords, source_weights, focus_steps, pupil_taps, blur_x, blur_y, blur_z
):
    devices = lax.axis_size("src")
    wide = layout_mask.shape[1] // devices
    local = jnp.concatenate([source_coords, source_weights[:, None]], axis=1)
    points = lax.all_gather(local, "src", axis=0, tiled=True)
    rows = padded_rows(pupil_taps, blur_x, blur_y)
    square = jax.ShapeDtypeStruct((256, 256), jnp.float32)
    limit = pltpu.CompilerParams(vmem_limit_bytes=48 * 2**20)
    intensity, along = pl.pallas_call(
        lambda *refs: image_kernel(pupil_taps.shape[0], *refs),
        out_shape=(square, square),
        in_specs=[smem, smem, vmem, vmem],
        out_specs=(vmem, vmem),
        scratch_shapes=table_scratch(),
        compiler_params=limit,
    )(points, focus_steps, layout_mask, rows)
    stack = lax.all_to_all(along, "src", 0, 0, tiled=True)
    mixed = pl.pallas_call(
        lambda *refs: stack_kernel(devices, wide, *refs),
        out_shape=square,
        in_specs=[smem, vmem, vmem],
        out_specs=vmem,
        scratch_shapes=[pltpu.VMEM((256, 256), jnp.float32)],
        compiler_params=limit,
    )(blur_z, stack, rows)
    latent = lax.all_to_all(mixed, "src", 0, 0, tiled=True).T
    return intensity, latent


def solution(mesh):
    in_specs = (P("groups", None), P("src", None), P("src"), P(), P(), P(), P(), P())
    out_specs = (P(("groups", "src"), None), P(("groups", "src"), None))
    body = plane_per_device if mesh.shape["src"] == 16 else on_device
    return jax.shard_map(
        body, mesh=mesh, in_specs=in_specs, out_specs=out_specs, check_vma=False
    )
```

```python
import math

import jax
import jax.numpy as jnp
from jax import lax
from jax.experimental import pallas as pl
from jax.experimental.pallas import tpu as pltpu
from jax.sharding import PartitionSpec as P

two_pi = 2.0 * math.pi
defocus_scale = 0.8
dose_scale = 2.0


def extended_2(block, sides, width):
    for axis, dim in sides:
        count = lax.axis_size(axis)
        forward = [(i, i + 1) for i in range(count - 1)]
        backward = [(target, source) for source, target in forward]
        low = lax.ppermute(
            lax.slice_in_dim(block, block.shape[dim] - width, None, axis=dim), axis, forward
        )
        high = lax.ppermute(lax.slice_in_dim(block, 0, width, axis=dim), axis, backward)
        block = jnp.concatenate([low, block, high], axis=dim)
    return block


def passed_along(block, axis, distance):
    devices = range(lax.axis_size(axis))
    route = [(i - distance, i) for i in devices if i - distance in devices]
    return lax.ppermute(block, axis, route)


def tap_matrix(out_pos, extent, tilt_index, focus_step, pupil_taps):
    tap_count = pupil_taps.shape[0]
    centre = (tap_count - 1) / 2.0
    column_pos = jnp.arange(extent, dtype=jnp.int32)
    offset = column_pos[None, :] - out_pos[:, None] + tap_count // 2
    inside = (offset >= 0) & (offset < tap_count)
    clipped = jnp.clip(offset, 0, tap_count - 1)
    amplitude = jnp.take(pupil_taps, clipped) / math.sqrt(tap_count)
    relative = clipped.astype(jnp.float32) - centre
    phase_angle = (
        two_pi * tilt_index.astype(jnp.float32) * relative / tap_count
        + defocus_scale * focus_step.astype(jnp.float32) * (relative / centre) ** 2
    )
    real_part = jnp.where(inside, amplitude * jnp.cos(phase_angle), jnp.zeros_like(amplitude))
    imag_part = jnp.where(inside, amplitude * jnp.sin(phase_angle), jnp.zeros_like(amplitude))
    return (real_part.astype(jnp.bfloat16), imag_part.astype(jnp.bfloat16))


def field_power(mask_bf, row_pos, tilt_x, tilt_y, focus_step, pupil_taps):
    rows_tile, cols_tile = mask_bf.shape
    row_count = row_pos.shape[0]
    col_pos = jnp.arange(cols_tile, dtype=jnp.int32)
    rows_real, rows_imag = tap_matrix(row_pos, rows_tile, tilt_y, focus_step, pupil_taps)
    cols_real, cols_imag = tap_matrix(col_pos, cols_tile, tilt_x, focus_step, pupil_taps)
    stacked = jnp.concatenate([rows_real, rows_imag], axis=0)
    first_pass = jnp.dot(stacked, mask_bf, preferred_element_type=jnp.float32).astype(jnp.bfloat16)
    joined = jnp.concatenate([first_pass[:row_count], first_pass[row_count:]], axis=1)
    upper_half = jnp.concatenate([cols_real.T, cols_imag.T], axis=1)
    lower_half = jnp.concatenate([-cols_imag.T, cols_real.T], axis=1)
    pupil_cols = jnp.concatenate([upper_half, lower_half], axis=0)
    field_parts = jnp.dot(joined, pupil_cols, preferred_element_type=jnp.float32)
    return field_parts[:, :cols_tile] ** 2 + field_parts[:, cols_tile:] ** 2


def on_device(
    layout_mask, source_coords, source_weights, focus_steps, pupil_taps, blur_x, blur_y, blur_z
):
    rows_tile, cols_tile = layout_mask.shape
    planes = focus_steps.shape[0]
    devices = lax.axis_size("src")
    src_local = source_coords.shape[0]
    mask_bf = layout_mask.astype(jnp.bfloat16)
    own_rows = planes * rows_tile // devices
    per_plane = devices // planes
    factors = source_weights.astype(jnp.float32) / (4.0 * src_local * devices)
    row_pos = jnp.arange(rows_tile, dtype=jnp.int32)

    def plane_term(focus_step):
        running = jnp.zeros((rows_tile, cols_tile), jnp.float32)
        for source in range(src_local):
            power = field_power(
                mask_bf,
                row_pos,
                source_coords[source, 0],
                source_coords[source, 1],
                focus_step,
                pupil_taps,
            )
            running = running + factors[source] * power
        return running

    partial_sum = lax.map(plane_term, focus_steps).reshape(planes * rows_tile, cols_tile)
    intensity = lax.psum_scatter(partial_sum, "src", scatter_dimension=0, tiled=True)
    acid_level = 1.0 - jnp.exp(-dose_scale * intensity)
    width_x = blur_x.shape[0]
    half_x = width_x // 2
    padded = jnp.pad(acid_level, ((0, 0), (half_x, half_x)))
    along_x = jnp.zeros_like(acid_level)
    for tap_index in range(width_x):
        along_x = (
            along_x + blur_x[tap_index] / width_x * padded[:, tap_index : tap_index + cols_tile]
        )
    width_y = blur_y.shape[0]
    half_y = width_y // 2
    extended = extended_2(along_x, (("src", 0),), half_y)
    along_y = jnp.zeros_like(along_x)
    for tap_index in range(width_y):
        along_y = along_y + blur_y[tap_index] / width_y * extended[tap_index : tap_index + own_rows]
    latent = blur_z[planes - 1] / planes * along_y
    for plane_lag in range(1 - planes, planes):
        if plane_lag != 0:
            arrived = passed_along(along_y, "src", plane_lag * per_plane)
            latent = latent + blur_z[plane_lag + planes - 1] / planes * arrived
    return (intensity, latent)


max_shift = 8
shifts = 2 * max_shift + 1
lanes = 512


def exact_dot(left, right):
    return jnp.dot(left, right, precision=lax.Precision.HIGHEST, preferred_element_type=jnp.float32)


def store_toeplitz(row, position, pieces):
    base = pltpu.roll(jnp.broadcast_to(row, (16, lanes)), position, 1, stride=1, stride_axis=0)
    for j in range(8):
        rolled = pltpu.roll(base, lanes - 128 + 16 * j, 1)
        for block, start in ((j + 8, 0), (j, 128)):
            part = rolled[:, start : start + 256]
            for ref, top, side, sign in pieces:
                value = part if sign > 0 else -part
                ref[top + 16 * block : top + 16 * block + 16, side : side + 256] = value.astype(
                    ref.dtype
                )


def store_taps(taps_ref, row, focus, flip, real_ref, imag_ref, tap_count):
    centre = (tap_count - 1) / 2.0
    amplitude = taps_ref[row : row + 1, :128] / math.sqrt(tap_count)
    shape = (24, 128)
    relative = (lax.broadcasted_iota(jnp.int32, shape, 1).astype(jnp.float32) - centre) * flip
    tilt = (lax.broadcasted_iota(jnp.int32, shape, 0) - max_shift).astype(jnp.float32)
    phase = (
        two_pi * tilt * relative / tap_count + defocus_scale * focus * (relative / centre) ** 2
    )
    real_ref[...] = jnp.zeros_like(real_ref)
    imag_ref[...] = jnp.zeros_like(imag_ref)
    real_ref[:, :128] = amplitude * jnp.cos(phase)
    imag_ref[:, :128] = amplitude * jnp.sin(phase)


def build_tables(tap_count, mask_ref, rows_ref, focus, tap_refs, stacked, fields, pupils):
    forward_real, forward_imag, back_real, back_imag = tap_refs
    store_taps(rows_ref, 0, focus, 1.0, forward_real, forward_imag, tap_count)
    store_taps(rows_ref, 1, focus, -1.0, back_real, back_imag, tap_count)
    mask_bf = mask_ref[...].astype(jnp.float32).astype(jnp.bfloat16)

    def one_shift(shift, carry):
        row = pl.ds(shift, 1)
        store_toeplitz(forward_real[row, :], 232, ((stacked, 0, 0, 1),))
        store_toeplitz(forward_imag[row, :], 232, ((stacked, 256, 0, 1),))
        first = jnp.dot(stacked[...], mask_bf, preferred_element_type=jnp.float32)
        fields[shift, :, :256] = first[:256].astype(jnp.bfloat16)
        fields[shift, :, 256:] = first[256:].astype(jnp.bfloat16)
        pupil = pupils.at[shift]
        store_toeplitz(back_real[row, :], 233, ((pupil, 0, 0, 1), (pupil, 256, 256, 1)))
        store_toeplitz(back_imag[row, :], 233, ((pupil, 0, 256, 1), (pupil, 256, 0, -1)))
        return carry

    lax.fori_loop(0, shifts, one_shift, 0)


def lane_row(count, value):
    lane = lax.broadcasted_iota(jnp.int32, (1, lanes), 1)
    row = jnp.zeros((1, lanes), jnp.float32)
    for t in range(count):
        row = jnp.where(lane == t, value(t), row)
    return row


def plane_kernel(
    n, wide, mask_ref, coords_ref, weights_ref, focus_ref, taps_ref, blur_x_ref, blur_y_ref,
    blur_z_ref, intensity_ref, latent_ref, rows, t0, t1, t2, t3, stacked, fields, pupils, blur,
    centre, mix, own, points, points_smem, along, columns, mixed, planes, send_sems, recv_sems,
    local_sem,
):
    me = lax.axis_index("src")
    group = lax.axis_index("groups")
    local = weights_ref.shape[0]
    tap_count, blur_count = taps_ref.shape[0], blur_x_ref.shape[0]
    barrier = pltpu.get_barrier_semaphore()

    def each(action):
        lax.fori_loop(1, n, lambda off, carry: (action(off), carry)[1], 0)

    def peer(off):
        return (group, lax.rem(me + off, n))

    def signal(off):
        pl.semaphore_signal(
            barrier, inc=1, device_id=peer(off), device_id_type=pl.DeviceIdType.MESH
        )

    def copy(phase, source, target, off, slot):
        return pltpu.make_async_remote_copy(
            src_ref=source(off),
            dst_ref=target.at[slot],
            send_sem=send_sems.at[phase, off],
            recv_sem=recv_sems.at[phase, off],
            device_id=peer(off),
            device_id_type=pl.DeviceIdType.MESH,
        )

    def start(phase, source, target):
        each(lambda off: copy(phase, source, target, off, me).start())

    def receive(phase, source, target):
        each(
            lambda off: copy(
                phase, source, target, off, lax.rem(me + n - off, n)
            ).wait_recv()
        )

    def sent(phase, source, target):
        each(lambda off: copy(phase, source, target, off, me).wait_send())

    each(signal)
    lane = lax.broadcasted_iota(jnp.int32, (1, 128), 1)
    packed = jnp.zeros((1, 128), jnp.int32)
    for s in range(local):
        packed = jnp.where(lane == 3 * s, coords_ref[s, 0], packed)
        packed = jnp.where(lane == 3 * s + 1, coords_ref[s, 1], packed)
        packed = jnp.where(lane == 3 * s + 2, weights_ref[s], packed)
    own[...] = packed
    points[me] = packed
    rows[0:1, :] = lane_row(tap_count, lambda t: taps_ref[t])
    rows[1:2, :] = lane_row(tap_count, lambda t: taps_ref[tap_count - 1 - t])
    rows[2:3, :] = lane_row(blur_count, lambda t: blur_x_ref[t] / blur_count)
    rows[3:4, :] = lane_row(blur_count, lambda t: blur_y_ref[blur_count - 1 - t] / blur_count)
    pl.semaphore_wait(barrier, n - 1)
    point_source = lambda off: own
    start(0, point_source, points)

    focus = focus_ref[me].astype(jnp.float32)
    build_tables(tap_count, mask_ref, rows, focus, (t0, t1, t2, t3), stacked, fields, pupils)
    store_toeplitz(rows[2:3, :], 241, ((blur, 0, 0, 1),))
    intensity_ref[...] = jnp.zeros_like(intensity_ref)
    receive(0, point_source, points)
    to_smem = pltpu.make_async_copy(points, points_smem, local_sem)
    to_smem.start()
    to_smem.wait()

    def one_device(device, carry):
        for s in range(local):
            point = [points_smem[device, 0, 3 * s + item] for item in range(3)]
            factor = point[2].astype(jnp.float32) / (4.0 * local * n)
            field = jnp.dot(
                fields[point[1] + max_shift],
                pupils[point[0] + max_shift],
                preferred_element_type=jnp.float32,
            )
            intensity_ref[...] += factor * (field[:, :256] ** 2 + field[:, 256:] ** 2)
        return carry

    lax.fori_loop(0, n, one_device, 0)
    acid = 1.0 - jnp.exp(-dose_scale * intensity_ref[...])
    along[...] = exact_dot(blur[...], acid.T).reshape(n, wide, 256)
    column_source = lambda off: along.at[lax.rem(me + off, n)]
    start(1, column_source, columns)
    columns[me] = along[me]

    back_y = rows[3:4, :]
    store_toeplitz(back_y, 241, ((centre, 0, 0, 1),))
    tall = jnp.broadcast_to(back_y, (16, lanes))
    before = pltpu.roll(tall, lanes - 31, 1, stride=1, stride_axis=0)[:, :256]
    after = pltpu.roll(tall, 241, 1, stride=1, stride_axis=0)[:, :256]
    pad = jnp.zeros((240, 256), jnp.float32)
    distance = lax.broadcasted_iota(jnp.int32, (256, 256), 0) - lax.broadcasted_iota(
        jnp.int32, (256, 256), 1
    )
    mix[...] = jnp.zeros_like(mix)
    for lag in range(1 - n, n):
        mix[...] = jnp.where(distance == lag * wide, blur_z_ref[lag + n - 1] / n, mix[...])

    receive(1, column_source, columns)
    stack = columns[...].reshape(256, 256)
    zero = jnp.zeros((wide, 256), jnp.float32)
    along_y = (
        exact_dot(stack, centre[...])
        + exact_dot(
            jnp.concatenate([zero, stack[:-wide]], axis=0), jnp.concatenate([pad, before], axis=0)
        )
        + exact_dot(
            jnp.concatenate([stack[wide:], zero], axis=0), jnp.concatenate([after, pad], axis=0)
        )
    )
    mixed[...] = exact_dot(mix[...], along_y).reshape(n, wide, 256)
    plane_source = lambda off: mixed.at[lax.rem(me + off, n)]
    start(2, plane_source, planes)
    planes[me] = mixed[me]
    sent(0, point_source, points)
    sent(1, column_source, columns)
    receive(2, plane_source, planes)
    latent_ref[...] = planes[...].reshape(256, 256).T
    sent(2, plane_source, planes)


def plane_per_device(
    layout_mask, source_coords, source_weights, focus_steps, pupil_taps, blur_x, blur_y, blur_z
):
    n = lax.axis_size("src")
    wide = layout_mask.shape[1] // n
    square = jax.ShapeDtypeStruct((256, 256), jnp.float32)
    full = pltpu.VMEM((256, 256), jnp.float32)
    parts = pltpu.VMEM((n, wide, 256), jnp.float32)
    vmem = pl.BlockSpec(memory_space=pltpu.VMEM)
    smem = pl.BlockSpec(memory_space=pltpu.SMEM)
    return pl.pallas_call(
        lambda *refs: plane_kernel(n, wide, *refs),
        out_shape=(square, square),
        in_specs=[vmem] + [smem] * 7,
        out_specs=(vmem, vmem),
        scratch_shapes=[pltpu.VMEM((8, lanes), jnp.float32)]
        + [pltpu.VMEM((24, lanes), jnp.float32)] * 4
        + [
            pltpu.VMEM((512, 256), jnp.bfloat16),
            pltpu.VMEM((shifts, 256, 512), jnp.bfloat16),
            pltpu.VMEM((shifts, 512, 512), jnp.bfloat16),
            full,
            full,
            full,
            pltpu.VMEM((1, 128), jnp.int32),
            pltpu.VMEM((n, 1, 128), jnp.int32),
            pltpu.SMEM((n, 1, 128), jnp.int32),
            parts,
            parts,
            parts,
            parts,
            pltpu.SemaphoreType.DMA((3, n)),
            pltpu.SemaphoreType.DMA((3, n)),
            pltpu.SemaphoreType.DMA,
        ],
        compiler_params=pltpu.CompilerParams(
            vmem_limit_bytes=48 * 2**20, collective_id=0, has_side_effects=True
        ),
    )(
        layout_mask, source_coords, source_weights, focus_steps, pupil_taps, blur_x, blur_y, blur_z
    )


def solution(mesh):
    in_specs = (P("groups", None), P("src", None), P("src"), P(), P(), P(), P(), P())
    out_specs = (P(("groups", "src"), None), P(("groups", "src"), None))
    body = plane_per_device if mesh.shape["src"] == 16 else on_device
    return jax.shard_map(
        body, mesh=mesh, in_specs=in_specs, out_specs=out_specs, check_vma=False
    )
```

```python
import math

import jax
import jax.numpy as jnp
from jax import lax
from jax.experimental import pallas as pl
from jax.experimental.pallas import tpu as pltpu
from jax.sharding import PartitionSpec as P

two_pi = 2.0 * math.pi
defocus_scale = 0.8
dose_scale = 2.0


def extended_2(block, sides, width):
    for axis, dim in sides:
        count = lax.axis_size(axis)
        forward = [(i, i + 1) for i in range(count - 1)]
        backward = [(target, source) for source, target in forward]
        low = lax.ppermute(
            lax.slice_in_dim(block, block.shape[dim] - width, None, axis=dim), axis, forward
        )
        high = lax.ppermute(lax.slice_in_dim(block, 0, width, axis=dim), axis, backward)
        block = jnp.concatenate([low, block, high], axis=dim)
    return block


def passed_along(block, axis, distance):
    devices = range(lax.axis_size(axis))
    route = [(i - distance, i) for i in devices if i - distance in devices]
    return lax.ppermute(block, axis, route)


def tap_matrix(out_pos, extent, tilt_index, focus_step, pupil_taps):
    tap_count = pupil_taps.shape[0]
    centre = (tap_count - 1) / 2.0
    column_pos = jnp.arange(extent, dtype=jnp.int32)
    offset = column_pos[None, :] - out_pos[:, None] + tap_count // 2
    inside = (offset >= 0) & (offset < tap_count)
    clipped = jnp.clip(offset, 0, tap_count - 1)
    amplitude = jnp.take(pupil_taps, clipped) / math.sqrt(tap_count)
    relative = clipped.astype(jnp.float32) - centre
    phase_angle = (
        two_pi * tilt_index.astype(jnp.float32) * relative / tap_count
        + defocus_scale * focus_step.astype(jnp.float32) * (relative / centre) ** 2
    )
    real_part = jnp.where(inside, amplitude * jnp.cos(phase_angle), jnp.zeros_like(amplitude))
    imag_part = jnp.where(inside, amplitude * jnp.sin(phase_angle), jnp.zeros_like(amplitude))
    return (real_part.astype(jnp.bfloat16), imag_part.astype(jnp.bfloat16))


def field_power(mask_bf, row_pos, tilt_x, tilt_y, focus_step, pupil_taps):
    rows_tile, cols_tile = mask_bf.shape
    row_count = row_pos.shape[0]
    col_pos = jnp.arange(cols_tile, dtype=jnp.int32)
    rows_real, rows_imag = tap_matrix(row_pos, rows_tile, tilt_y, focus_step, pupil_taps)
    cols_real, cols_imag = tap_matrix(col_pos, cols_tile, tilt_x, focus_step, pupil_taps)
    stacked = jnp.concatenate([rows_real, rows_imag], axis=0)
    first_pass = jnp.dot(stacked, mask_bf, preferred_element_type=jnp.float32).astype(jnp.bfloat16)
    joined = jnp.concatenate([first_pass[:row_count], first_pass[row_count:]], axis=1)
    upper_half = jnp.concatenate([cols_real.T, cols_imag.T], axis=1)
    lower_half = jnp.concatenate([-cols_imag.T, cols_real.T], axis=1)
    pupil_cols = jnp.concatenate([upper_half, lower_half], axis=0)
    field_parts = jnp.dot(joined, pupil_cols, preferred_element_type=jnp.float32)
    return field_parts[:, :cols_tile] ** 2 + field_parts[:, cols_tile:] ** 2


def on_device(
    layout_mask, source_coords, source_weights, focus_steps, pupil_taps, blur_x, blur_y, blur_z
):
    rows_tile, cols_tile = layout_mask.shape
    planes = focus_steps.shape[0]
    devices = lax.axis_size("src")
    src_local = source_coords.shape[0]
    mask_bf = layout_mask.astype(jnp.bfloat16)
    own_rows = planes * rows_tile // devices
    per_plane = devices // planes
    factors = source_weights.astype(jnp.float32) / (4.0 * src_local * devices)
    row_pos = jnp.arange(rows_tile, dtype=jnp.int32)

    def plane_term(focus_step):
        running = jnp.zeros((rows_tile, cols_tile), jnp.float32)
        for source in range(src_local):
            power = field_power(
                mask_bf,
                row_pos,
                source_coords[source, 0],
                source_coords[source, 1],
                focus_step,
                pupil_taps,
            )
            running = running + factors[source] * power
        return running

    partial_sum = lax.map(plane_term, focus_steps).reshape(planes * rows_tile, cols_tile)
    intensity = lax.psum_scatter(partial_sum, "src", scatter_dimension=0, tiled=True)
    acid_level = 1.0 - jnp.exp(-dose_scale * intensity)
    width_x = blur_x.shape[0]
    half_x = width_x // 2
    padded = jnp.pad(acid_level, ((0, 0), (half_x, half_x)))
    along_x = jnp.zeros_like(acid_level)
    for tap_index in range(width_x):
        along_x = (
            along_x + blur_x[tap_index] / width_x * padded[:, tap_index : tap_index + cols_tile]
        )
    width_y = blur_y.shape[0]
    half_y = width_y // 2
    extended = extended_2(along_x, (("src", 0),), half_y)
    along_y = jnp.zeros_like(along_x)
    for tap_index in range(width_y):
        along_y = along_y + blur_y[tap_index] / width_y * extended[tap_index : tap_index + own_rows]
    latent = blur_z[planes - 1] / planes * along_y
    for plane_lag in range(1 - planes, planes):
        if plane_lag != 0:
            arrived = passed_along(along_y, "src", plane_lag * per_plane)
            latent = latent + blur_z[plane_lag + planes - 1] / planes * arrived
    return (intensity, latent)


max_shift = 8
shifts = 2 * max_shift + 1
lanes = 512


def exact_dot(left, right):
    def halves(value):
        high = value.astype(jnp.bfloat16)
        return high, (value - high.astype(jnp.float32)).astype(jnp.bfloat16)

    def product(a, b):
        return jnp.dot(a, b, preferred_element_type=jnp.float32)

    left_high, left_low = halves(left)
    right_high, right_low = halves(right)
    return (
        product(left_high, right_low) + product(left_low, right_high)
    ) + product(left_high, right_high)


def store_toeplitz(row, position, pieces):
    base = pltpu.roll(jnp.broadcast_to(row, (16, lanes)), position, 1, stride=1, stride_axis=0)
    for j in range(8):
        rolled = pltpu.roll(base, lanes - 128 + 16 * j, 1)
        for block, start in ((j + 8, 0), (j, 128)):
            part = rolled[:, start : start + 256]
            for ref, top, side, sign in pieces:
                value = part if sign > 0 else -part
                ref[top + 16 * block : top + 16 * block + 16, side : side + 256] = value.astype(
                    ref.dtype
                )


def store_taps(taps_ref, row, focus, flip, real_ref, imag_ref, tap_count):
    centre = (tap_count - 1) / 2.0
    amplitude = taps_ref[row : row + 1, :128] / math.sqrt(tap_count)
    shape = (24, 128)
    relative = (lax.broadcasted_iota(jnp.int32, shape, 1).astype(jnp.float32) - centre) * flip
    tilt = (lax.broadcasted_iota(jnp.int32, shape, 0) - max_shift).astype(jnp.float32)
    phase = (
        two_pi * tilt * relative / tap_count + defocus_scale * focus * (relative / centre) ** 2
    )
    real_ref[...] = jnp.zeros_like(real_ref)
    imag_ref[...] = jnp.zeros_like(imag_ref)
    real_ref[:, :128] = amplitude * jnp.cos(phase)
    imag_ref[:, :128] = amplitude * jnp.sin(phase)


def build_tables(tap_count, mask_ref, rows_ref, focus, tap_refs, stacked, fields, pupils):
    forward_real, forward_imag, back_real, back_imag = tap_refs
    store_taps(rows_ref, 0, focus, 1.0, forward_real, forward_imag, tap_count)
    store_taps(rows_ref, 1, focus, -1.0, back_real, back_imag, tap_count)
    mask_bf = mask_ref[...].astype(jnp.float32).astype(jnp.bfloat16)

    def one_shift(shift, carry):
        row = pl.ds(shift, 1)
        store_toeplitz(forward_real[row, :], 232, ((stacked, 0, 0, 1),))
        store_toeplitz(forward_imag[row, :], 232, ((stacked, 256, 0, 1),))
        first = jnp.dot(stacked[...], mask_bf, preferred_element_type=jnp.float32)
        fields[shift, :, :256] = first[:256].astype(jnp.bfloat16)
        fields[shift, :, 256:] = first[256:].astype(jnp.bfloat16)
        pupil = pupils.at[shift]
        store_toeplitz(back_real[row, :], 233, ((pupil, 0, 0, 1), (pupil, 256, 256, 1)))
        store_toeplitz(back_imag[row, :], 233, ((pupil, 0, 256, 1), (pupil, 256, 0, -1)))
        return carry

    lax.fori_loop(0, shifts, one_shift, 0)


def lane_row(count, value):
    lane = lax.broadcasted_iota(jnp.int32, (1, lanes), 1)
    row = jnp.zeros((1, lanes), jnp.float32)
    for t in range(count):
        row = jnp.where(lane == t, value(t), row)
    return row


def plane_kernel(
    n, wide, mask_hbm, coords_hbm, weights_hbm, focus_hbm, taps_hbm, blur_x_hbm, blur_y_hbm,
    blur_z_hbm, intensity_ref, latent_ref, mask_ref, coords_ref, weights_ref, focus_ref, taps_ref,
    blur_x_ref, blur_y_ref, blur_z_ref, arg_sems, rows, t0, t1, t2, t3, stacked, fields, pupils, blur,
    centre, mix, own, points, points_smem, along, columns, mixed, planes, send_sems, recv_sems,
    local_sem,
):
    me = lax.axis_index("src")
    group = lax.axis_index("groups")
    local = weights_ref.shape[0]
    tap_count, blur_count = taps_ref.shape[0], blur_x_ref.shape[0]
    barrier = pltpu.get_barrier_semaphore()

    def each(action):
        lax.fori_loop(1, n, lambda off, carry: (action(off), carry)[1], 0)

    def peer(off):
        return (group, lax.rem(me + off, n))

    def signal(off):
        pl.semaphore_signal(
            barrier, inc=1, device_id=peer(off), device_id_type=pl.DeviceIdType.MESH
        )

    def copy(phase, source, target, off, slot):
        return pltpu.make_async_remote_copy(
            src_ref=source(off),
            dst_ref=target.at[slot],
            send_sem=send_sems.at[phase, off],
            recv_sem=recv_sems.at[phase, off],
            device_id=peer(off),
            device_id_type=pl.DeviceIdType.MESH,
        )

    def start(phase, source, target):
        each(lambda off: copy(phase, source, target, off, me).start())

    def receive(phase, source, target):
        each(
            lambda off: copy(
                phase, source, target, off, lax.rem(me + n - off, n)
            ).wait_recv()
        )

    def sent(phase, source, target):
        each(lambda off: copy(phase, source, target, off, me).wait_send())

    fetches = [
        pltpu.make_async_copy(source, target, arg_sems.at[place])
        for place, (source, target) in enumerate(
            (
                (coords_hbm, coords_ref),
                (weights_hbm, weights_ref),
                (focus_hbm, focus_ref),
                (taps_hbm, taps_ref),
                (blur_x_hbm, blur_x_ref),
                (blur_y_hbm, blur_y_ref),
                (blur_z_hbm, blur_z_ref),
                (mask_hbm, mask_ref),
            )
        )
    ]
    for fetch in fetches:
        fetch.start()
    each(signal)
    for fetch in fetches:
        fetch.wait()
    lane = lax.broadcasted_iota(jnp.int32, (1, 128), 1)
    packed = jnp.zeros((1, 128), jnp.int32)
    for s in range(local):
        packed = jnp.where(lane == 3 * s, coords_ref[s, 0], packed)
        packed = jnp.where(lane == 3 * s + 1, coords_ref[s, 1], packed)
        packed = jnp.where(lane == 3 * s + 2, weights_ref[s], packed)
    own[...] = packed
    points[me] = packed
    rows[0:1, :] = lane_row(tap_count, lambda t: taps_ref[t])
    rows[1:2, :] = lane_row(tap_count, lambda t: taps_ref[tap_count - 1 - t])
    rows[2:3, :] = lane_row(blur_count, lambda t: blur_x_ref[t] / blur_count)
    rows[3:4, :] = lane_row(blur_count, lambda t: blur_y_ref[blur_count - 1 - t] / blur_count)
    pl.semaphore_wait(barrier, n - 1)
    point_source = lambda off: own
    start(0, point_source, points)

    focus = focus_ref[me].astype(jnp.float32)
    build_tables(tap_count, mask_ref, rows, focus, (t0, t1, t2, t3), stacked, fields, pupils)
    store_toeplitz(rows[2:3, :], 241, ((blur, 0, 0, 1),))
    intensity_ref[...] = jnp.zeros_like(intensity_ref)
    receive(0, point_source, points)
    to_smem = pltpu.make_async_copy(points, points_smem, local_sem)
    to_smem.start()
    to_smem.wait()

    def one_device(device, carry):
        for s in range(local):
            point = [points_smem[device, 0, 3 * s + item] for item in range(3)]
            factor = point[2].astype(jnp.float32) / (4.0 * local * n)
            field = jnp.dot(
                fields[point[1] + max_shift],
                pupils[point[0] + max_shift],
                preferred_element_type=jnp.float32,
            )
            intensity_ref[...] += factor * (field[:, :256] ** 2 + field[:, 256:] ** 2)
        return carry

    lax.fori_loop(0, n, one_device, 0)
    acid = 1.0 - jnp.exp(-dose_scale * intensity_ref[...])
    along[...] = exact_dot(blur[...], acid.T).reshape(n, wide, 256)
    column_source = lambda off: along.at[lax.rem(me + off, n)]
    start(1, column_source, columns)
    columns[me] = along[me]

    back_y = rows[3:4, :]
    store_toeplitz(back_y, 241, ((centre, 0, 0, 1),))
    tall = jnp.broadcast_to(back_y, (16, lanes))
    before = pltpu.roll(tall, lanes - 31, 1, stride=1, stride_axis=0)[:, :256]
    after = pltpu.roll(tall, 241, 1, stride=1, stride_axis=0)[:, :256]
    pad = jnp.zeros((112, 256), jnp.float32)
    distance = lax.broadcasted_iota(jnp.int32, (256, 256), 0) - lax.broadcasted_iota(
        jnp.int32, (256, 256), 1
    )
    mix[...] = jnp.zeros_like(mix)
    for lag in range(1 - n, n):
        mix[...] = jnp.where(distance == lag * wide, blur_z_ref[lag + n - 1] / n, mix[...])

    receive(1, column_source, columns)
    stack = columns[...].reshape(256, 256)
    zero = jnp.zeros((wide, 128), jnp.float32)
    along_y = (
        exact_dot(stack, centre[...])
        + exact_dot(
            jnp.concatenate([zero, stack[:-wide, 128:]], axis=0),
            jnp.concatenate([pad, before], axis=0),
        )
        + exact_dot(
            jnp.concatenate([stack[wide:, :128], zero], axis=0),
            jnp.concatenate([after, pad], axis=0),
        )
    )
    mixed[...] = exact_dot(mix[...], along_y).reshape(n, wide, 256)
    plane_source = lambda off: mixed.at[lax.rem(me + off, n)]
    start(2, plane_source, planes)
    planes[me] = mixed[me]
    sent(0, point_source, points)
    sent(1, column_source, columns)
    receive(2, plane_source, planes)
    latent_ref[...] = planes[...].reshape(256, 256).T
    sent(2, plane_source, planes)


def plane_per_device(
    layout_mask, source_coords, source_weights, focus_steps, pupil_taps, blur_x, blur_y, blur_z
):
    n = lax.axis_size("src")
    wide = layout_mask.shape[1] // n
    square = jax.ShapeDtypeStruct((256, 256), jnp.float32)
    full = pltpu.VMEM((256, 256), jnp.float32)
    parts = pltpu.VMEM((n, wide, 256), jnp.float32)
    vmem = pl.BlockSpec(memory_space=pltpu.VMEM)
    hbm = pl.BlockSpec(memory_space=pltpu.HBM)
    arguments = (
        source_coords, source_weights, focus_steps, pupil_taps, blur_x, blur_y, blur_z
    )
    return pl.pallas_call(
        lambda *refs: plane_kernel(n, wide, *refs),
        out_shape=(square, square),
        in_specs=[hbm] * 8,
        out_specs=(vmem, vmem),
        scratch_shapes=[pltpu.VMEM((256, 256), jnp.int32)]
        + [pltpu.SMEM(value.shape, value.dtype) for value in arguments]
        + [pltpu.SemaphoreType.DMA((8,)), pltpu.VMEM((8, lanes), jnp.float32)]
        + [pltpu.VMEM((24, lanes), jnp.float32)] * 4
        + [
            pltpu.VMEM((512, 256), jnp.bfloat16),
            pltpu.VMEM((shifts, 256, 512), jnp.bfloat16),
            pltpu.VMEM((shifts, 512, 512), jnp.bfloat16),
            full,
            full,
            full,
            pltpu.VMEM((1, 128), jnp.int32),
            pltpu.VMEM((n, 1, 128), jnp.int32),
            pltpu.SMEM((n, 1, 128), jnp.int32),
            parts,
            parts,
            parts,
            parts,
            pltpu.SemaphoreType.DMA((3, n)),
            pltpu.SemaphoreType.DMA((3, n)),
            pltpu.SemaphoreType.DMA,
        ],
        compiler_params=pltpu.CompilerParams(
            vmem_limit_bytes=64 * 2**20 - 2**17, collective_id=0, has_side_effects=True
        ),
    )(layout_mask, *arguments)


def solution(mesh):
    in_specs = (P("groups", None), P("src", None), P("src"), P(), P(), P(), P(), P())
    out_specs = (P(("groups", "src"), None), P(("groups", "src"), None))
    body = plane_per_device if mesh.shape["src"] == 16 else on_device
    return jax.shard_map(
        body, mesh=mesh, in_specs=in_specs, out_specs=out_specs, check_vma=False
    )
```

```python
import math

import jax
import jax.numpy as jnp
from jax import lax
from jax.experimental import pallas as pl
from jax.experimental.pallas import tpu as pltpu
from jax.sharding import PartitionSpec as P

two_pi = 2.0 * math.pi
defocus_scale = 0.8
dose_scale = 2.0


def extended_2(block, sides, width):
    for axis, dim in sides:
        count = lax.axis_size(axis)
        forward = [(i, i + 1) for i in range(count - 1)]
        backward = [(target, source) for source, target in forward]
        low = lax.ppermute(
            lax.slice_in_dim(block, block.shape[dim] - width, None, axis=dim), axis, forward
        )
        high = lax.ppermute(lax.slice_in_dim(block, 0, width, axis=dim), axis, backward)
        block = jnp.concatenate([low, block, high], axis=dim)
    return block


def passed_along(block, axis, distance):
    devices = range(lax.axis_size(axis))
    route = [(i - distance, i) for i in devices if i - distance in devices]
    return lax.ppermute(block, axis, route)


def tap_matrix(out_pos, extent, tilt_index, focus_step, pupil_taps):
    tap_count = pupil_taps.shape[0]
    centre = (tap_count - 1) / 2.0
    column_pos = jnp.arange(extent, dtype=jnp.int32)
    offset = column_pos[None, :] - out_pos[:, None] + tap_count // 2
    inside = (offset >= 0) & (offset < tap_count)
    clipped = jnp.clip(offset, 0, tap_count - 1)
    amplitude = jnp.take(pupil_taps, clipped) / math.sqrt(tap_count)
    relative = clipped.astype(jnp.float32) - centre
    phase_angle = (
        two_pi * tilt_index.astype(jnp.float32) * relative / tap_count
        + defocus_scale * focus_step.astype(jnp.float32) * (relative / centre) ** 2
    )
    real_part = jnp.where(inside, amplitude * jnp.cos(phase_angle), jnp.zeros_like(amplitude))
    imag_part = jnp.where(inside, amplitude * jnp.sin(phase_angle), jnp.zeros_like(amplitude))
    return (real_part.astype(jnp.bfloat16), imag_part.astype(jnp.bfloat16))


def field_power(mask_bf, row_pos, tilt_x, tilt_y, focus_step, pupil_taps):
    rows_tile, cols_tile = mask_bf.shape
    row_count = row_pos.shape[0]
    col_pos = jnp.arange(cols_tile, dtype=jnp.int32)
    rows_real, rows_imag = tap_matrix(row_pos, rows_tile, tilt_y, focus_step, pupil_taps)
    cols_real, cols_imag = tap_matrix(col_pos, cols_tile, tilt_x, focus_step, pupil_taps)
    stacked = jnp.concatenate([rows_real, rows_imag], axis=0)
    first_pass = jnp.dot(stacked, mask_bf, preferred_element_type=jnp.float32).astype(jnp.bfloat16)
    joined = jnp.concatenate([first_pass[:row_count], first_pass[row_count:]], axis=1)
    upper_half = jnp.concatenate([cols_real.T, cols_imag.T], axis=1)
    lower_half = jnp.concatenate([-cols_imag.T, cols_real.T], axis=1)
    pupil_cols = jnp.concatenate([upper_half, lower_half], axis=0)
    field_parts = jnp.dot(joined, pupil_cols, preferred_element_type=jnp.float32)
    return field_parts[:, :cols_tile] ** 2 + field_parts[:, cols_tile:] ** 2


def on_device(
    layout_mask, source_coords, source_weights, focus_steps, pupil_taps, blur_x, blur_y, blur_z
):
    rows_tile, cols_tile = layout_mask.shape
    planes = focus_steps.shape[0]
    devices = lax.axis_size("src")
    src_local = source_coords.shape[0]
    mask_bf = layout_mask.astype(jnp.bfloat16)
    own_rows = planes * rows_tile // devices
    per_plane = devices // planes
    factors = source_weights.astype(jnp.float32) / (4.0 * src_local * devices)
    row_pos = jnp.arange(rows_tile, dtype=jnp.int32)

    def plane_term(focus_step):
        running = jnp.zeros((rows_tile, cols_tile), jnp.float32)
        for source in range(src_local):
            power = field_power(
                mask_bf,
                row_pos,
                source_coords[source, 0],
                source_coords[source, 1],
                focus_step,
                pupil_taps,
            )
            running = running + factors[source] * power
        return running

    partial_sum = lax.map(plane_term, focus_steps).reshape(planes * rows_tile, cols_tile)
    intensity = lax.psum_scatter(partial_sum, "src", scatter_dimension=0, tiled=True)
    acid_level = 1.0 - jnp.exp(-dose_scale * intensity)
    width_x = blur_x.shape[0]
    half_x = width_x // 2
    padded = jnp.pad(acid_level, ((0, 0), (half_x, half_x)))
    along_x = jnp.zeros_like(acid_level)
    for tap_index in range(width_x):
        along_x = (
            along_x + blur_x[tap_index] / width_x * padded[:, tap_index : tap_index + cols_tile]
        )
    width_y = blur_y.shape[0]
    half_y = width_y // 2
    extended = extended_2(along_x, (("src", 0),), half_y)
    along_y = jnp.zeros_like(along_x)
    for tap_index in range(width_y):
        along_y = along_y + blur_y[tap_index] / width_y * extended[tap_index : tap_index + own_rows]
    latent = blur_z[planes - 1] / planes * along_y
    for plane_lag in range(1 - planes, planes):
        if plane_lag != 0:
            arrived = passed_along(along_y, "src", plane_lag * per_plane)
            latent = latent + blur_z[plane_lag + planes - 1] / planes * arrived
    return (intensity, latent)


max_shift = 8
shifts = 2 * max_shift + 1
lanes = 512


def exact_dot(left, right):
    def halves(value):
        high = value.astype(jnp.bfloat16)
        return high, (value - high.astype(jnp.float32)).astype(jnp.bfloat16)

    def product(a, b):
        return jnp.dot(a, b, preferred_element_type=jnp.float32)

    left_high, left_low = halves(left)
    right_high, right_low = halves(right)
    return (
        product(left_high, right_low) + product(left_low, right_high)
    ) + product(left_high, right_high)


def store_toeplitz(row, position, pieces):
    base = pltpu.roll(jnp.broadcast_to(row, (16, lanes)), position, 1, stride=1, stride_axis=0)
    for j in range(8):
        rolled = pltpu.roll(base, lanes - 128 + 16 * j, 1)
        for block, start in ((j + 8, 0), (j, 128)):
            part = rolled[:, start : start + 256]
            for ref, top, side, sign in pieces:
                value = part if sign > 0 else -part
                ref[top + 16 * block : top + 16 * block + 16, side : side + 256] = value.astype(
                    ref.dtype
                )


def store_taps(taps_ref, row, focus, flip, real_ref, imag_ref, tap_count):
    centre = (tap_count - 1) / 2.0
    amplitude = taps_ref[row : row + 1, :128] / math.sqrt(tap_count)
    shape = (24, 128)
    relative = (lax.broadcasted_iota(jnp.int32, shape, 1).astype(jnp.float32) - centre) * flip
    tilt = (lax.broadcasted_iota(jnp.int32, shape, 0) - max_shift).astype(jnp.float32)
    phase = (
        two_pi * tilt * relative / tap_count + defocus_scale * focus * (relative / centre) ** 2
    )
    real_ref[...] = jnp.zeros_like(real_ref)
    imag_ref[...] = jnp.zeros_like(imag_ref)
    real_ref[:, :128] = amplitude * jnp.cos(phase)
    imag_ref[:, :128] = amplitude * jnp.sin(phase)


def build_tables(tap_count, mask_ref, rows_ref, focus, tap_refs, stacked_slots, fields, pupils):
    forward_real, forward_imag, back_real, back_imag = tap_refs
    store_taps(rows_ref, 0, focus, 1.0, forward_real, forward_imag, tap_count)
    store_taps(rows_ref, 1, focus, -1.0, back_real, back_imag, tap_count)
    mask_bf = mask_ref[...].astype(jnp.float32).astype(jnp.bfloat16)

    def one_shift(shift, slot):
        stacked = stacked_slots.at[slot]
        row = pl.ds(shift, 1)
        store_toeplitz(forward_real[row, :], 232, ((stacked, 0, 0, 1),))
        store_toeplitz(forward_imag[row, :], 232, ((stacked, 256, 0, 1),))
        first = jnp.dot(stacked[...], mask_bf, preferred_element_type=jnp.float32)
        fields[shift, :, :256] = first[:256].astype(jnp.bfloat16)
        fields[shift, :, 256:] = first[256:].astype(jnp.bfloat16)
        pupil = pupils.at[shift]
        store_toeplitz(back_real[row, :], 233, ((pupil, 0, 0, 1), (pupil, 256, 256, 1)))
        store_toeplitz(back_imag[row, :], 233, ((pupil, 0, 256, 1), (pupil, 256, 0, -1)))

    def two_shifts(pair, carry):
        one_shift(2 * pair, 0)
        one_shift(2 * pair + 1, 1)
        return carry

    lax.fori_loop(0, shifts // 2, two_shifts, 0)
    one_shift(shifts - 1, 0)


def lane_row(count, value):
    lane = lax.broadcasted_iota(jnp.int32, (1, lanes), 1)
    row = jnp.zeros((1, lanes), jnp.float32)
    for t in range(count):
        row = jnp.where(lane == t, value(t), row)
    return row


def plane_kernel(
    n, wide, mask_hbm, coords_hbm, weights_hbm, focus_hbm, taps_hbm, blur_x_hbm, blur_y_hbm,
    blur_z_hbm, intensity_ref, latent_ref, mask_ref, coords_ref, weights_ref, focus_ref, taps_ref,
    blur_x_ref, blur_y_ref, blur_z_ref, arg_sems, rows, t0, t1, t2, t3, stacked, fields, pupils, blur,
    centre, mix, own, points, points_smem, along, columns, mixed, planes, send_sems, recv_sems,
    local_sem,
):
    me = lax.axis_index("src")
    group = lax.axis_index("groups")
    local = weights_ref.shape[0]
    tap_count, blur_count = taps_ref.shape[0], blur_x_ref.shape[0]
    barrier = pltpu.get_barrier_semaphore()

    def each(action):
        lax.fori_loop(1, n, lambda off, carry: (action(off), carry)[1], 0)

    def peer(off):
        return (group, lax.rem(me + off, n))

    def signal(off):
        pl.semaphore_signal(
            barrier, inc=1, device_id=peer(off), device_id_type=pl.DeviceIdType.MESH
        )

    def copy(phase, source, target, off, slot):
        return pltpu.make_async_remote_copy(
            src_ref=source(off),
            dst_ref=target.at[slot],
            send_sem=send_sems.at[phase, off],
            recv_sem=recv_sems.at[phase, off],
            device_id=peer(off),
            device_id_type=pl.DeviceIdType.MESH,
        )

    def start(phase, source, target):
        each(lambda off: copy(phase, source, target, off, me).start())

    def receive(phase, source, target):
        each(
            lambda off: copy(
                phase, source, target, off, lax.rem(me + n - off, n)
            ).wait_recv()
        )

    def sent(phase, source, target):
        each(lambda off: copy(phase, source, target, off, me).wait_send())

    fetches = [
        pltpu.make_async_copy(source, target, arg_sems.at[place])
        for place, (source, target) in enumerate(
            (
                (coords_hbm, coords_ref),
                (weights_hbm, weights_ref),
                (focus_hbm, focus_ref),
                (taps_hbm, taps_ref),
                (blur_x_hbm, blur_x_ref),
                (blur_y_hbm, blur_y_ref),
                (blur_z_hbm, blur_z_ref),
                (mask_hbm, mask_ref),
            )
        )
    ]
    for fetch in fetches:
        fetch.start()
    each(signal)
    for fetch in fetches:
        fetch.wait()
    lane = lax.broadcasted_iota(jnp.int32, (1, 128), 1)
    packed = jnp.zeros((1, 128), jnp.int32)
    for s in range(local):
        packed = jnp.where(lane == 3 * s, coords_ref[s, 0], packed)
        packed = jnp.where(lane == 3 * s + 1, coords_ref[s, 1], packed)
        packed = jnp.where(lane == 3 * s + 2, weights_ref[s], packed)
    own[...] = packed
    points[me] = packed
    rows[0:1, :] = lane_row(tap_count, lambda t: taps_ref[t])
    rows[1:2, :] = lane_row(tap_count, lambda t: taps_ref[tap_count - 1 - t])
    rows[2:3, :] = lane_row(blur_count, lambda t: blur_x_ref[t] / blur_count)
    rows[3:4, :] = lane_row(blur_count, lambda t: blur_y_ref[blur_count - 1 - t] / blur_count)
    pl.semaphore_wait(barrier, n - 1)
    point_source = lambda off: own
    start(0, point_source, points)

    focus = focus_ref[me].astype(jnp.float32)
    build_tables(tap_count, mask_ref, rows, focus, (t0, t1, t2, t3), stacked, fields, pupils)
    store_toeplitz(rows[2:3, :], 241, ((blur, 0, 0, 1),))
    intensity_ref[...] = jnp.zeros_like(intensity_ref)
    receive(0, point_source, points)
    to_smem = pltpu.make_async_copy(points, points_smem, local_sem)
    to_smem.start()
    to_smem.wait()

    def two_devices(pair, carry):
        power = jnp.zeros((256, 256), jnp.float32)
        for place in range(2 * local):
            device, s = 2 * pair + place // local, place % local
            point = [points_smem[device, 0, 3 * s + item] for item in range(3)]
            factor = point[2].astype(jnp.float32) / (4.0 * local * n)
            field = jnp.dot(
                fields[point[1] + max_shift],
                pupils[point[0] + max_shift],
                preferred_element_type=jnp.float32,
            )
            power = power + factor * (field[:, :256] ** 2 + field[:, 256:] ** 2)
        intensity_ref[...] += power
        return carry

    lax.fori_loop(0, n // 2, two_devices, 0)
    acid = 1.0 - jnp.exp(-dose_scale * intensity_ref[...])
    along[...] = exact_dot(blur[...], acid.T).reshape(n, wide, 256)
    column_source = lambda off: along.at[lax.rem(me + off, n)]
    start(1, column_source, columns)
    columns[me] = along[me]

    back_y = rows[3:4, :]
    store_toeplitz(back_y, 241, ((centre, 0, 0, 1),))
    tall = jnp.broadcast_to(back_y, (16, lanes))
    before = pltpu.roll(tall, lanes - 31, 1, stride=1, stride_axis=0)[:, :256]
    after = pltpu.roll(tall, 241, 1, stride=1, stride_axis=0)[:, :256]
    pad = jnp.zeros((112, 256), jnp.float32)
    distance = lax.broadcasted_iota(jnp.int32, (256, 256), 0) - lax.broadcasted_iota(
        jnp.int32, (256, 256), 1
    )
    mix[...] = jnp.zeros_like(mix)
    for lag in range(1 - n, n):
        mix[...] = jnp.where(distance == lag * wide, blur_z_ref[lag + n - 1] / n, mix[...])

    receive(1, column_source, columns)
    stack = columns[...].reshape(256, 256)
    zero = jnp.zeros((wide, 128), jnp.float32)
    along_y = (
        exact_dot(stack, centre[...])
        + exact_dot(
            jnp.concatenate([zero, stack[:-wide, 128:]], axis=0),
            jnp.concatenate([pad, before], axis=0),
        )
        + exact_dot(
            jnp.concatenate([stack[wide:, :128], zero], axis=0),
            jnp.concatenate([after, pad], axis=0),
        )
    )
    mixed[...] = exact_dot(mix[...], along_y).reshape(n, wide, 256)
    plane_source = lambda off: mixed.at[lax.rem(me + off, n)]
    start(2, plane_source, planes)
    planes[me] = mixed[me]
    sent(0, point_source, points)
    sent(1, column_source, columns)
    receive(2, plane_source, planes)
    latent_ref[...] = planes[...].reshape(256, 256).T
    sent(2, plane_source, planes)


def plane_per_device(
    layout_mask, source_coords, source_weights, focus_steps, pupil_taps, blur_x, blur_y, blur_z
):
    n = lax.axis_size("src")
    wide = layout_mask.shape[1] // n
    square = jax.ShapeDtypeStruct((256, 256), jnp.float32)
    full = pltpu.VMEM((256, 256), jnp.float32)
    parts = pltpu.VMEM((n, wide, 256), jnp.float32)
    vmem = pl.BlockSpec(memory_space=pltpu.VMEM)
    hbm = pl.BlockSpec(memory_space=pltpu.HBM)
    arguments = (
        source_coords, source_weights, focus_steps, pupil_taps, blur_x, blur_y, blur_z
    )
    return pl.pallas_call(
        lambda *refs: plane_kernel(n, wide, *refs),
        out_shape=(square, square),
        in_specs=[hbm] * 8,
        out_specs=(vmem, vmem),
        scratch_shapes=[pltpu.VMEM((256, 256), jnp.int32)]
        + [pltpu.SMEM(value.shape, value.dtype) for value in arguments]
        + [pltpu.SemaphoreType.DMA((8,)), pltpu.VMEM((8, lanes), jnp.float32)]
        + [pltpu.VMEM((24, lanes), jnp.float32)] * 4
        + [
            pltpu.VMEM((2, 512, 256), jnp.bfloat16),
            pltpu.VMEM((shifts, 256, 512), jnp.bfloat16),
            pltpu.VMEM((shifts, 512, 512), jnp.bfloat16),
            full,
            full,
            full,
            pltpu.VMEM((1, 128), jnp.int32),
            pltpu.VMEM((n, 1, 128), jnp.int32),
            pltpu.SMEM((n, 1, 128), jnp.int32),
            parts,
            parts,
            parts,
            parts,
            pltpu.SemaphoreType.DMA((3, n)),
            pltpu.SemaphoreType.DMA((3, n)),
            pltpu.SemaphoreType.DMA,
        ],
        compiler_params=pltpu.CompilerParams(
            vmem_limit_bytes=64 * 2**20 - 2**17, collective_id=0, has_side_effects=True
        ),
    )(layout_mask, *arguments)


def solution(mesh):
    in_specs = (P("groups", None), P("src", None), P("src"), P(), P(), P(), P(), P())
    out_specs = (P(("groups", "src"), None), P(("groups", "src"), None))
    body = plane_per_device if mesh.shape["src"] == 16 else on_device
    return jax.shard_map(
        body, mesh=mesh, in_specs=in_specs, out_specs=out_specs, check_vma=False
    )
```

```python
import math

import jax
import jax.numpy as jnp
from jax import lax
from jax.experimental import pallas as pl
from jax.experimental.pallas import tpu as pltpu
from jax.sharding import PartitionSpec as P

two_pi = 2.0 * math.pi
defocus_scale = 0.8
dose_scale = 2.0


def extended_2(block, sides, width):
    for axis, dim in sides:
        count = lax.axis_size(axis)
        forward = [(i, i + 1) for i in range(count - 1)]
        backward = [(target, source) for source, target in forward]
        low = lax.ppermute(
            lax.slice_in_dim(block, block.shape[dim] - width, None, axis=dim), axis, forward
        )
        high = lax.ppermute(lax.slice_in_dim(block, 0, width, axis=dim), axis, backward)
        block = jnp.concatenate([low, block, high], axis=dim)
    return block


def passed_along(block, axis, distance):
    devices = range(lax.axis_size(axis))
    route = [(i - distance, i) for i in devices if i - distance in devices]
    return lax.ppermute(block, axis, route)


def tap_matrix(out_pos, extent, tilt_index, focus_step, pupil_taps):
    tap_count = pupil_taps.shape[0]
    centre = (tap_count - 1) / 2.0
    column_pos = jnp.arange(extent, dtype=jnp.int32)
    offset = column_pos[None, :] - out_pos[:, None] + tap_count // 2
    inside = (offset >= 0) & (offset < tap_count)
    clipped = jnp.clip(offset, 0, tap_count - 1)
    amplitude = jnp.take(pupil_taps, clipped) / math.sqrt(tap_count)
    relative = clipped.astype(jnp.float32) - centre
    phase_angle = (
        two_pi * tilt_index.astype(jnp.float32) * relative / tap_count
        + defocus_scale * focus_step.astype(jnp.float32) * (relative / centre) ** 2
    )
    real_part = jnp.where(inside, amplitude * jnp.cos(phase_angle), jnp.zeros_like(amplitude))
    imag_part = jnp.where(inside, amplitude * jnp.sin(phase_angle), jnp.zeros_like(amplitude))
    return (real_part.astype(jnp.bfloat16), imag_part.astype(jnp.bfloat16))


def field_power(mask_bf, row_pos, tilt_x, tilt_y, focus_step, pupil_taps):
    rows_tile, cols_tile = mask_bf.shape
    row_count = row_pos.shape[0]
    col_pos = jnp.arange(cols_tile, dtype=jnp.int32)
    rows_real, rows_imag = tap_matrix(row_pos, rows_tile, tilt_y, focus_step, pupil_taps)
    cols_real, cols_imag = tap_matrix(col_pos, cols_tile, tilt_x, focus_step, pupil_taps)
    stacked = jnp.concatenate([rows_real, rows_imag], axis=0)
    first_pass = jnp.dot(stacked, mask_bf, preferred_element_type=jnp.float32).astype(jnp.bfloat16)
    joined = jnp.concatenate([first_pass[:row_count], first_pass[row_count:]], axis=1)
    upper_half = jnp.concatenate([cols_real.T, cols_imag.T], axis=1)
    lower_half = jnp.concatenate([-cols_imag.T, cols_real.T], axis=1)
    pupil_cols = jnp.concatenate([upper_half, lower_half], axis=0)
    field_parts = jnp.dot(joined, pupil_cols, preferred_element_type=jnp.float32)
    return field_parts[:, :cols_tile] ** 2 + field_parts[:, cols_tile:] ** 2


def on_device(
    layout_mask, source_coords, source_weights, focus_steps, pupil_taps, blur_x, blur_y, blur_z
):
    rows_tile, cols_tile = layout_mask.shape
    planes = focus_steps.shape[0]
    devices = lax.axis_size("src")
    src_local = source_coords.shape[0]
    mask_bf = layout_mask.astype(jnp.bfloat16)
    own_rows = planes * rows_tile // devices
    per_plane = devices // planes
    factors = source_weights.astype(jnp.float32) / (4.0 * src_local * devices)
    row_pos = jnp.arange(rows_tile, dtype=jnp.int32)

    def plane_term(focus_step):
        running = jnp.zeros((rows_tile, cols_tile), jnp.float32)
        for source in range(src_local):
            power = field_power(
                mask_bf,
                row_pos,
                source_coords[source, 0],
                source_coords[source, 1],
                focus_step,
                pupil_taps,
            )
            running = running + factors[source] * power
        return running

    partial_sum = lax.map(plane_term, focus_steps).reshape(planes * rows_tile, cols_tile)
    intensity = lax.psum_scatter(partial_sum, "src", scatter_dimension=0, tiled=True)
    acid_level = 1.0 - jnp.exp(-dose_scale * intensity)
    width_x = blur_x.shape[0]
    half_x = width_x // 2
    padded = jnp.pad(acid_level, ((0, 0), (half_x, half_x)))
    along_x = jnp.zeros_like(acid_level)
    for tap_index in range(width_x):
        along_x = (
            along_x + blur_x[tap_index] / width_x * padded[:, tap_index : tap_index + cols_tile]
        )
    width_y = blur_y.shape[0]
    half_y = width_y // 2
    extended = extended_2(along_x, (("src", 0),), half_y)
    along_y = jnp.zeros_like(along_x)
    for tap_index in range(width_y):
        along_y = along_y + blur_y[tap_index] / width_y * extended[tap_index : tap_index + own_rows]
    latent = blur_z[planes - 1] / planes * along_y
    for plane_lag in range(1 - planes, planes):
        if plane_lag != 0:
            arrived = passed_along(along_y, "src", plane_lag * per_plane)
            latent = latent + blur_z[plane_lag + planes - 1] / planes * arrived
    return (intensity, latent)


max_shift = 8
shifts = 2 * max_shift + 1
lanes = 512


def exact_dot(left, right):
    def halves(value):
        high = value.astype(jnp.bfloat16)
        return high, (value - high.astype(jnp.float32)).astype(jnp.bfloat16)

    def product(a, b):
        return jnp.dot(a, b, preferred_element_type=jnp.float32)

    left_high, left_low = halves(left)
    right_high, right_low = halves(right)
    return (
        product(left_high, right_low) + product(left_low, right_high)
    ) + product(left_high, right_high)


def store_toeplitz(row, position, pieces):
    base = pltpu.roll(jnp.broadcast_to(row, (16, lanes)), position, 1, stride=1, stride_axis=0)
    for j in range(8):
        rolled = pltpu.roll(base, lanes - 128 + 16 * j, 1)
        for block, start in ((j + 8, 0), (j, 128)):
            part = rolled[:, start : start + 256]
            for ref, top, side, sign in pieces:
                value = part if sign > 0 else -part
                ref[top + 16 * block : top + 16 * block + 16, side : side + 256] = value.astype(
                    ref.dtype
                )


def store_taps(taps_ref, row, focus, flip, real_ref, imag_ref, tap_count):
    centre = (tap_count - 1) / 2.0
    amplitude = taps_ref[row : row + 1, :128] / math.sqrt(tap_count)
    shape = (24, 128)
    relative = (lax.broadcasted_iota(jnp.int32, shape, 1).astype(jnp.float32) - centre) * flip
    tilt = (lax.broadcasted_iota(jnp.int32, shape, 0) - max_shift).astype(jnp.float32)
    phase = (
        two_pi * tilt * relative / tap_count + defocus_scale * focus * (relative / centre) ** 2
    )
    real_ref[...] = jnp.zeros_like(real_ref)
    imag_ref[...] = jnp.zeros_like(imag_ref)
    real_ref[:, :128] = amplitude * jnp.cos(phase)
    imag_ref[:, :128] = amplitude * jnp.sin(phase)


def build_tables(tap_count, mask_ref, rows_ref, focus, tap_refs, stacked_slots, fields, pupils):
    forward_real, forward_imag, back_real, back_imag = tap_refs
    store_taps(rows_ref, 0, focus, 1.0, forward_real, forward_imag, tap_count)
    store_taps(rows_ref, 1, focus, -1.0, back_real, back_imag, tap_count)
    mask_bf = mask_ref[...].astype(jnp.float32).astype(jnp.bfloat16)

    def one_shift(shift, slot):
        stacked = stacked_slots.at[slot]
        row = pl.ds(shift, 1)
        store_toeplitz(forward_real[row, :], 232, ((stacked, 0, 0, 1),))
        store_toeplitz(forward_imag[row, :], 232, ((stacked, 256, 0, 1),))
        first = jnp.dot(stacked[...], mask_bf, preferred_element_type=jnp.float32)
        fields[shift, :, :256] = first[:256].astype(jnp.bfloat16)
        fields[shift, :, 256:] = first[256:].astype(jnp.bfloat16)
        pupil = pupils.at[shift]
        store_toeplitz(back_real[row, :], 233, ((pupil, 0, 0, 1), (pupil, 256, 256, 1)))
        store_toeplitz(back_imag[row, :], 233, ((pupil, 0, 256, 1), (pupil, 256, 0, -1)))

    def four_shifts(step, carry):
        for slot in range(4):
            one_shift(4 * step + slot, slot)
        return carry

    lax.fori_loop(0, shifts // 4, four_shifts, 0)
    one_shift(shifts - 1, 0)


def lane_row(count, value):
    lane = lax.broadcasted_iota(jnp.int32, (1, lanes), 1)
    row = jnp.zeros((1, lanes), jnp.float32)
    for t in range(count):
        row = jnp.where(lane == t, value(t), row)
    return row


def plane_kernel(
    n, wide, mask_hbm, coords_hbm, weights_hbm, focus_hbm, taps_hbm, blur_x_hbm, blur_y_hbm,
    blur_z_hbm, intensity_ref, latent_ref, mask_ref, coords_ref, weights_ref, focus_ref, taps_ref,
    blur_x_ref, blur_y_ref, blur_z_ref, arg_sems, rows, t0, t1, t2, t3, stacked, fields, pupils, blur,
    centre, mix, own, points, points_smem, along, columns, mixed, planes, send_sems, recv_sems,
    local_sem,
):
    me = lax.axis_index("src")
    group = lax.axis_index("groups")
    local = weights_ref.shape[0]
    tap_count, blur_count = taps_ref.shape[0], blur_x_ref.shape[0]
    barrier = pltpu.get_barrier_semaphore()

    def each(action):
        lax.fori_loop(1, n, lambda off, carry: (action(off), carry)[1], 0)

    def peer(off):
        return (group, lax.rem(me + off, n))

    def signal(off):
        pl.semaphore_signal(
            barrier, inc=1, device_id=peer(off), device_id_type=pl.DeviceIdType.MESH
        )

    def copy(phase, source, target, off, slot):
        return pltpu.make_async_remote_copy(
            src_ref=source(off),
            dst_ref=target.at[slot],
            send_sem=send_sems.at[phase, off],
            recv_sem=recv_sems.at[phase, off],
            device_id=peer(off),
            device_id_type=pl.DeviceIdType.MESH,
        )

    def start(phase, source, target):
        each(lambda off: copy(phase, source, target, off, me).start())

    def receive(phase, source, target):
        each(
            lambda off: copy(
                phase, source, target, off, lax.rem(me + n - off, n)
            ).wait_recv()
        )

    def sent(phase, source, target):
        each(lambda off: copy(phase, source, target, off, me).wait_send())

    fetches = [
        pltpu.make_async_copy(source, target, arg_sems.at[place])
        for place, (source, target) in enumerate(
            (
                (coords_hbm, coords_ref),
                (weights_hbm, weights_ref),
                (focus_hbm, focus_ref),
                (taps_hbm, taps_ref),
                (blur_x_hbm, blur_x_ref),
                (blur_y_hbm, blur_y_ref),
                (blur_z_hbm, blur_z_ref),
                (mask_hbm, mask_ref),
            )
        )
    ]
    for fetch in fetches:
        fetch.start()
    each(signal)
    for fetch in fetches:
        fetch.wait()
    lane = lax.broadcasted_iota(jnp.int32, (1, 128), 1)
    packed = jnp.zeros((1, 128), jnp.int32)
    for s in range(local):
        packed = jnp.where(lane == 3 * s, coords_ref[s, 0], packed)
        packed = jnp.where(lane == 3 * s + 1, coords_ref[s, 1], packed)
        packed = jnp.where(lane == 3 * s + 2, weights_ref[s], packed)
    own[...] = packed
    points[me] = packed
    rows[0:1, :] = lane_row(tap_count, lambda t: taps_ref[t])
    rows[1:2, :] = lane_row(tap_count, lambda t: taps_ref[tap_count - 1 - t])
    rows[2:3, :] = lane_row(blur_count, lambda t: blur_x_ref[t] / blur_count)
    rows[3:4, :] = lane_row(blur_count, lambda t: blur_y_ref[blur_count - 1 - t] / blur_count)
    pl.semaphore_wait(barrier, n - 1)
    point_source = lambda off: own
    start(0, point_source, points)

    focus = focus_ref[me].astype(jnp.float32)
    build_tables(tap_count, mask_ref, rows, focus, (t0, t1, t2, t3), stacked, fields, pupils)
    store_toeplitz(rows[2:3, :], 241, ((blur, 0, 0, 1),))
    intensity_ref[...] = jnp.zeros_like(intensity_ref)
    receive(0, point_source, points)
    to_smem = pltpu.make_async_copy(points, points_smem, local_sem)
    to_smem.start()
    to_smem.wait()

    def four_devices(step, carry):
        power = jnp.zeros((256, 256), jnp.float32)
        for place in range(4 * local):
            device, s = 4 * step + place // local, place % local
            point = [points_smem[device, 0, 3 * s + item] for item in range(3)]
            factor = point[2].astype(jnp.float32) / (4.0 * local * n)
            field = jnp.dot(
                fields[point[1] + max_shift],
                pupils[point[0] + max_shift],
                preferred_element_type=jnp.float32,
            )
            power = power + factor * (field[:, :256] ** 2 + field[:, 256:] ** 2)
        intensity_ref[...] += power
        return carry

    lax.fori_loop(0, n // 4, four_devices, 0)
    acid = 1.0 - jnp.exp(-dose_scale * intensity_ref[...])
    along[...] = exact_dot(blur[...], acid.T).reshape(n, wide, 256)
    column_source = lambda off: along.at[lax.rem(me + off, n)]
    start(1, column_source, columns)
    columns[me] = along[me]

    back_y = rows[3:4, :]
    store_toeplitz(back_y, 241, ((centre, 0, 0, 1),))
    tall = jnp.broadcast_to(back_y, (16, lanes))
    before = pltpu.roll(tall, lanes - 31, 1, stride=1, stride_axis=0)[:, :256]
    after = pltpu.roll(tall, 241, 1, stride=1, stride_axis=0)[:, :256]
    pad = jnp.zeros((112, 256), jnp.float32)
    distance = lax.broadcasted_iota(jnp.int32, (256, 256), 0) - lax.broadcasted_iota(
        jnp.int32, (256, 256), 1
    )
    mix[...] = jnp.zeros_like(mix)
    for lag in range(1 - n, n):
        mix[...] = jnp.where(distance == lag * wide, blur_z_ref[lag + n - 1] / n, mix[...])

    receive(1, column_source, columns)
    stack = columns[...].reshape(256, 256)
    zero = jnp.zeros((wide, 128), jnp.float32)
    along_y = (
        exact_dot(stack, centre[...])
        + exact_dot(
            jnp.concatenate([zero, stack[:-wide, 128:]], axis=0),
            jnp.concatenate([pad, before], axis=0),
        )
        + exact_dot(
            jnp.concatenate([stack[wide:, :128], zero], axis=0),
            jnp.concatenate([after, pad], axis=0),
        )
    )
    mixed[...] = exact_dot(mix[...], along_y).reshape(n, wide, 256)
    plane_source = lambda off: mixed.at[lax.rem(me + off, n)]
    start(2, plane_source, planes)
    planes[me] = mixed[me]
    sent(0, point_source, points)
    sent(1, column_source, columns)
    receive(2, plane_source, planes)
    latent_ref[...] = planes[...].reshape(256, 256).T
    sent(2, plane_source, planes)


def plane_per_device(
    layout_mask, source_coords, source_weights, focus_steps, pupil_taps, blur_x, blur_y, blur_z
):
    n = lax.axis_size("src")
    wide = layout_mask.shape[1] // n
    square = jax.ShapeDtypeStruct((256, 256), jnp.float32)
    full = pltpu.VMEM((256, 256), jnp.float32)
    parts = pltpu.VMEM((n, wide, 256), jnp.float32)
    vmem = pl.BlockSpec(memory_space=pltpu.VMEM)
    hbm = pl.BlockSpec(memory_space=pltpu.HBM)
    arguments = (
        source_coords, source_weights, focus_steps, pupil_taps, blur_x, blur_y, blur_z
    )
    return pl.pallas_call(
        lambda *refs: plane_kernel(n, wide, *refs),
        out_shape=(square, square),
        in_specs=[hbm] * 8,
        out_specs=(vmem, vmem),
        scratch_shapes=[pltpu.VMEM((256, 256), jnp.int32)]
        + [pltpu.SMEM(value.shape, value.dtype) for value in arguments]
        + [pltpu.SemaphoreType.DMA((8,)), pltpu.VMEM((8, lanes), jnp.float32)]
        + [pltpu.VMEM((24, lanes), jnp.float32)] * 4
        + [
            pltpu.VMEM((4, 512, 256), jnp.bfloat16),
            pltpu.VMEM((shifts, 256, 512), jnp.bfloat16),
            pltpu.VMEM((shifts, 512, 512), jnp.bfloat16),
            full,
            full,
            full,
            pltpu.VMEM((1, 128), jnp.int32),
            pltpu.VMEM((n, 1, 128), jnp.int32),
            pltpu.SMEM((n, 1, 128), jnp.int32),
            parts,
            parts,
            parts,
            parts,
            pltpu.SemaphoreType.DMA((3, n)),
            pltpu.SemaphoreType.DMA((3, n)),
            pltpu.SemaphoreType.DMA,
        ],
        compiler_params=pltpu.CompilerParams(
            vmem_limit_bytes=64 * 2**20 - 2**17, collective_id=0, has_side_effects=True
        ),
    )(layout_mask, *arguments)


def solution(mesh):
    in_specs = (P("groups", None), P("src", None), P("src"), P(), P(), P(), P(), P())
    out_specs = (P(("groups", "src"), None), P(("groups", "src"), None))
    body = plane_per_device if mesh.shape["src"] == 16 else on_device
    return jax.shard_map(
        body, mesh=mesh, in_specs=in_specs, out_specs=out_specs, check_vma=False
    )
```

```python
import math

import jax
import jax.numpy as jnp
from jax import lax
from jax.experimental import pallas as pl
from jax.experimental.pallas import tpu as pltpu
from jax.sharding import PartitionSpec as P

two_pi = 2.0 * math.pi
defocus_scale = 0.8
dose_scale = 2.0


def extended_2(block, sides, width):
    for axis, dim in sides:
        count = lax.axis_size(axis)
        forward = [(i, i + 1) for i in range(count - 1)]
        backward = [(target, source) for source, target in forward]
        low = lax.ppermute(
            lax.slice_in_dim(block, block.shape[dim] - width, None, axis=dim), axis, forward
        )
        high = lax.ppermute(lax.slice_in_dim(block, 0, width, axis=dim), axis, backward)
        block = jnp.concatenate([low, block, high], axis=dim)
    return block


def passed_along(block, axis, distance):
    devices = range(lax.axis_size(axis))
    route = [(i - distance, i) for i in devices if i - distance in devices]
    return lax.ppermute(block, axis, route)


def tap_matrix(out_pos, extent, tilt_index, focus_step, pupil_taps):
    tap_count = pupil_taps.shape[0]
    centre = (tap_count - 1) / 2.0
    column_pos = jnp.arange(extent, dtype=jnp.int32)
    offset = column_pos[None, :] - out_pos[:, None] + tap_count // 2
    inside = (offset >= 0) & (offset < tap_count)
    clipped = jnp.clip(offset, 0, tap_count - 1)
    amplitude = jnp.take(pupil_taps, clipped) / math.sqrt(tap_count)
    relative = clipped.astype(jnp.float32) - centre
    phase_angle = (
        two_pi * tilt_index.astype(jnp.float32) * relative / tap_count
        + defocus_scale * focus_step.astype(jnp.float32) * (relative / centre) ** 2
    )
    real_part = jnp.where(inside, amplitude * jnp.cos(phase_angle), jnp.zeros_like(amplitude))
    imag_part = jnp.where(inside, amplitude * jnp.sin(phase_angle), jnp.zeros_like(amplitude))
    return (real_part.astype(jnp.bfloat16), imag_part.astype(jnp.bfloat16))


def field_power(mask_bf, row_pos, tilt_x, tilt_y, focus_step, pupil_taps):
    rows_tile, cols_tile = mask_bf.shape
    row_count = row_pos.shape[0]
    col_pos = jnp.arange(cols_tile, dtype=jnp.int32)
    rows_real, rows_imag = tap_matrix(row_pos, rows_tile, tilt_y, focus_step, pupil_taps)
    cols_real, cols_imag = tap_matrix(col_pos, cols_tile, tilt_x, focus_step, pupil_taps)
    stacked = jnp.concatenate([rows_real, rows_imag], axis=0)
    first_pass = jnp.dot(stacked, mask_bf, preferred_element_type=jnp.float32).astype(jnp.bfloat16)
    joined = jnp.concatenate([first_pass[:row_count], first_pass[row_count:]], axis=1)
    upper_half = jnp.concatenate([cols_real.T, cols_imag.T], axis=1)
    lower_half = jnp.concatenate([-cols_imag.T, cols_real.T], axis=1)
    pupil_cols = jnp.concatenate([upper_half, lower_half], axis=0)
    field_parts = jnp.dot(joined, pupil_cols, preferred_element_type=jnp.float32)
    return field_parts[:, :cols_tile] ** 2 + field_parts[:, cols_tile:] ** 2


def on_device(
    layout_mask, source_coords, source_weights, focus_steps, pupil_taps, blur_x, blur_y, blur_z
):
    rows_tile, cols_tile = layout_mask.shape
    planes = focus_steps.shape[0]
    devices = lax.axis_size("src")
    src_local = source_coords.shape[0]
    mask_bf = layout_mask.astype(jnp.bfloat16)
    own_rows = planes * rows_tile // devices
    per_plane = devices // planes
    factors = source_weights.astype(jnp.float32) / (4.0 * src_local * devices)
    row_pos = jnp.arange(rows_tile, dtype=jnp.int32)

    def plane_term(focus_step):
        running = jnp.zeros((rows_tile, cols_tile), jnp.float32)
        for source in range(src_local):
            power = field_power(
                mask_bf,
                row_pos,
                source_coords[source, 0],
                source_coords[source, 1],
                focus_step,
                pupil_taps,
            )
            running = running + factors[source] * power
        return running

    partial_sum = lax.map(plane_term, focus_steps).reshape(planes * rows_tile, cols_tile)
    intensity = lax.psum_scatter(partial_sum, "src", scatter_dimension=0, tiled=True)
    acid_level = 1.0 - jnp.exp(-dose_scale * intensity)
    width_x = blur_x.shape[0]
    half_x = width_x // 2
    padded = jnp.pad(acid_level, ((0, 0), (half_x, half_x)))
    along_x = jnp.zeros_like(acid_level)
    for tap_index in range(width_x):
        along_x = (
            along_x + blur_x[tap_index] / width_x * padded[:, tap_index : tap_index + cols_tile]
        )
    width_y = blur_y.shape[0]
    half_y = width_y // 2
    extended = extended_2(along_x, (("src", 0),), half_y)
    along_y = jnp.zeros_like(along_x)
    for tap_index in range(width_y):
        along_y = along_y + blur_y[tap_index] / width_y * extended[tap_index : tap_index + own_rows]
    latent = blur_z[planes - 1] / planes * along_y
    for plane_lag in range(1 - planes, planes):
        if plane_lag != 0:
            arrived = passed_along(along_y, "src", plane_lag * per_plane)
            latent = latent + blur_z[plane_lag + planes - 1] / planes * arrived
    return (intensity, latent)


max_shift = 8
shifts = 2 * max_shift + 1
lanes = 512


def exact_dot(left, right):
    def halves(value):
        high = value.astype(jnp.bfloat16)
        return high, (value - high.astype(jnp.float32)).astype(jnp.bfloat16)

    def product(a, b):
        return jnp.dot(a, b, preferred_element_type=jnp.float32)

    left_high, left_low = halves(left)
    right_high, right_low = halves(right)
    return (
        product(left_high, right_low) + product(left_low, right_high)
    ) + product(left_high, right_high)


def store_toeplitz(row, position, pieces):
    base = pltpu.roll(jnp.broadcast_to(row, (16, 128)), 0, 1, stride=1, stride_axis=0)
    lane = lax.broadcasted_iota(jnp.int32, (16, 128), 1)
    zero = jnp.zeros((16, 128), jnp.float32)
    for j in range(8):
        first = 16 * j + position - 256
        turn, tile = first % 128, first // 128
        rolled = pltpu.roll(base, turn, 1) if turn else base
        wraps = turn > 65
        kept = jnp.where(lane >= turn, rolled, zero) if wraps else rolled
        wrapped = jnp.where(lane < turn, rolled, zero) if wraps else zero
        for block, start in ((j, tile), (j + 8, tile + 1)):
            for column in range(2):
                part = kept if column == start else wrapped if column == start + 1 else zero
                for ref, top, side, sign in pieces:
                    value = part if sign > 0 else -part
                    left = side + 128 * column
                    ref[top + 16 * block : top + 16 * block + 16, left : left + 128] = (
                        value.astype(ref.dtype)
                    )


def store_taps(taps_ref, row, focus, flip, real_ref, imag_ref, tap_count):
    centre = (tap_count - 1) / 2.0
    amplitude = taps_ref[row : row + 1, :128] / math.sqrt(tap_count)
    shape = (24, 128)
    relative = (lax.broadcasted_iota(jnp.int32, shape, 1).astype(jnp.float32) - centre) * flip
    tilt = (lax.broadcasted_iota(jnp.int32, shape, 0) - max_shift).astype(jnp.float32)
    phase = (
        two_pi * tilt * relative / tap_count + defocus_scale * focus * (relative / centre) ** 2
    )
    real_ref[...] = amplitude * jnp.cos(phase)
    imag_ref[...] = amplitude * jnp.sin(phase)


def build_tables(tap_count, mask_ref, rows_ref, focus, tap_refs, stacked_slots, fields, pupils):
    forward_real, forward_imag, back_real, back_imag = tap_refs
    store_taps(rows_ref, 0, focus, 1.0, forward_real, forward_imag, tap_count)
    store_taps(rows_ref, 1, focus, -1.0, back_real, back_imag, tap_count)
    mask_bf = mask_ref[...].astype(jnp.float32).astype(jnp.bfloat16)

    def one_shift(shift, slot):
        stacked = stacked_slots.at[slot]
        row = pl.ds(shift, 1)
        store_toeplitz(forward_real[row, :], 232, ((stacked, 0, 0, 1),))
        store_toeplitz(forward_imag[row, :], 232, ((stacked, 256, 0, 1),))
        first = jnp.dot(stacked[...], mask_bf, preferred_element_type=jnp.float32)
        fields[shift, :, :256] = first[:256].astype(jnp.bfloat16)
        fields[shift, :, 256:] = first[256:].astype(jnp.bfloat16)
        pupil = pupils.at[shift]
        store_toeplitz(back_real[row, :], 233, ((pupil, 0, 0, 1), (pupil, 256, 256, 1)))
        store_toeplitz(back_imag[row, :], 233, ((pupil, 0, 256, 1), (pupil, 256, 0, -1)))

    def four_shifts(step, carry):
        for slot in range(4):
            one_shift(4 * step + slot, slot)
        return carry

    lax.fori_loop(0, shifts // 4, four_shifts, 0)
    one_shift(shifts - 1, 0)


def lane_row(count, value):
    lane = lax.broadcasted_iota(jnp.int32, (1, lanes), 1)
    row = jnp.zeros((1, lanes), jnp.float32)
    for t in range(count):
        row = jnp.where(lane == t, value(t), row)
    return row


def plane_kernel(
    n, wide, mask_hbm, coords_hbm, weights_hbm, focus_hbm, taps_hbm, blur_x_hbm, blur_y_hbm,
    blur_z_hbm, intensity_ref, latent_ref, mask_ref, coords_ref, weights_ref, focus_ref, taps_ref,
    blur_x_ref, blur_y_ref, blur_z_ref, arg_sems, rows, t0, t1, t2, t3, stacked, fields, pupils, blur,
    centre, mix, own, points, points_smem, along, columns, mixed, planes, send_sems, recv_sems,
    local_sem,
):
    me = lax.axis_index("src")
    group = lax.axis_index("groups")
    local = weights_ref.shape[0]
    tap_count, blur_count = taps_ref.shape[0], blur_x_ref.shape[0]
    barrier = pltpu.get_barrier_semaphore()

    def each(action):
        lax.fori_loop(1, n, lambda off, carry: (action(off), carry)[1], 0)

    def peer(off):
        return (group, lax.rem(me + off, n))

    def signal(off):
        pl.semaphore_signal(
            barrier, inc=1, device_id=peer(off), device_id_type=pl.DeviceIdType.MESH
        )

    def copy(phase, source, target, off, slot):
        return pltpu.make_async_remote_copy(
            src_ref=source(off),
            dst_ref=target.at[slot],
            send_sem=send_sems.at[phase, off],
            recv_sem=recv_sems.at[phase, off],
            device_id=peer(off),
            device_id_type=pl.DeviceIdType.MESH,
        )

    def start(phase, source, target):
        each(lambda off: copy(phase, source, target, off, me).start())

    def receive(phase, source, target):
        each(
            lambda off: copy(
                phase, source, target, off, lax.rem(me + n - off, n)
            ).wait_recv()
        )

    def sent(phase, source, target):
        each(lambda off: copy(phase, source, target, off, me).wait_send())

    fetches = [
        pltpu.make_async_copy(source, target, arg_sems.at[place])
        for place, (source, target) in enumerate(
            (
                (coords_hbm, coords_ref),
                (weights_hbm, weights_ref),
                (focus_hbm, focus_ref),
                (taps_hbm, taps_ref),
                (blur_x_hbm, blur_x_ref),
                (blur_y_hbm, blur_y_ref),
                (blur_z_hbm, blur_z_ref),
                (mask_hbm, mask_ref),
            )
        )
    ]
    for fetch in fetches:
        fetch.start()
    each(signal)
    for fetch in fetches:
        fetch.wait()
    lane = lax.broadcasted_iota(jnp.int32, (1, 128), 1)
    packed = jnp.zeros((1, 128), jnp.int32)
    for s in range(local):
        packed = jnp.where(lane == 3 * s, coords_ref[s, 0], packed)
        packed = jnp.where(lane == 3 * s + 1, coords_ref[s, 1], packed)
        packed = jnp.where(lane == 3 * s + 2, weights_ref[s], packed)
    own[...] = packed
    points[me] = packed
    rows[0:1, :] = lane_row(tap_count, lambda t: taps_ref[t])
    rows[1:2, :] = lane_row(tap_count, lambda t: taps_ref[tap_count - 1 - t])
    rows[2:3, :] = lane_row(blur_count, lambda t: blur_x_ref[t] / blur_count)
    rows[3:4, :] = lane_row(blur_count, lambda t: blur_y_ref[blur_count - 1 - t] / blur_count)
    pl.semaphore_wait(barrier, n - 1)
    point_source = lambda off: own
    start(0, point_source, points)

    focus = focus_ref[me].astype(jnp.float32)
    build_tables(tap_count, mask_ref, rows, focus, (t0, t1, t2, t3), stacked, fields, pupils)
    store_toeplitz(rows[2:3, :128], 241, ((blur, 0, 0, 1),))
    intensity_ref[...] = jnp.zeros_like(intensity_ref)
    receive(0, point_source, points)
    to_smem = pltpu.make_async_copy(points, points_smem, local_sem)
    to_smem.start()
    to_smem.wait()

    def four_devices(step, carry):
        power = jnp.zeros((256, 256), jnp.float32)
        for place in range(4 * local):
            device, s = 4 * step + place // local, place % local
            point = [points_smem[device, 0, 3 * s + item] for item in range(3)]
            factor = point[2].astype(jnp.float32) / (4.0 * local * n)
            field = jnp.dot(
                fields[point[1] + max_shift],
                pupils[point[0] + max_shift],
                preferred_element_type=jnp.float32,
            )
            power = power + factor * (field[:, :256] ** 2 + field[:, 256:] ** 2)
        intensity_ref[...] += power
        return carry

    lax.fori_loop(0, n // 4, four_devices, 0)
    acid = 1.0 - jnp.exp(-dose_scale * intensity_ref[...])
    along[...] = exact_dot(blur[...], acid.T).reshape(n, wide, 256)
    column_source = lambda off: along.at[lax.rem(me + off, n)]
    start(1, column_source, columns)
    columns[me] = along[me]

    back_y = rows[3:4, :]
    store_toeplitz(rows[3:4, :128], 241, ((centre, 0, 0, 1),))
    tall = jnp.broadcast_to(back_y, (16, lanes))
    before = pltpu.roll(tall, lanes - 31, 1, stride=1, stride_axis=0)[:, :256]
    after = pltpu.roll(tall, 241, 1, stride=1, stride_axis=0)[:, :256]
    pad = jnp.zeros((112, 256), jnp.float32)
    distance = lax.broadcasted_iota(jnp.int32, (256, 256), 0) - lax.broadcasted_iota(
        jnp.int32, (256, 256), 1
    )
    mix[...] = jnp.zeros_like(mix)
    for lag in range(1 - n, n):
        mix[...] = jnp.where(distance == lag * wide, blur_z_ref[lag + n - 1] / n, mix[...])

    receive(1, column_source, columns)
    stack = columns[...].reshape(256, 256)
    zero = jnp.zeros((wide, 128), jnp.float32)
    along_y = (
        exact_dot(stack, centre[...])
        + exact_dot(
            jnp.concatenate([zero, stack[:-wide, 128:]], axis=0),
            jnp.concatenate([pad, before], axis=0),
        )
        + exact_dot(
            jnp.concatenate([stack[wide:, :128], zero], axis=0),
            jnp.concatenate([after, pad], axis=0),
        )
    )
    mixed[...] = exact_dot(mix[...], along_y).reshape(n, wide, 256)
    plane_source = lambda off: mixed.at[lax.rem(me + off, n)]
    start(2, plane_source, planes)
    planes[me] = mixed[me]
    sent(0, point_source, points)
    sent(1, column_source, columns)
    receive(2, plane_source, planes)
    latent_ref[...] = planes[...].reshape(256, 256).T
    sent(2, plane_source, planes)


def plane_per_device(
    layout_mask, source_coords, source_weights, focus_steps, pupil_taps, blur_x, blur_y, blur_z
):
    n = lax.axis_size("src")
    wide = layout_mask.shape[1] // n
    square = jax.ShapeDtypeStruct((256, 256), jnp.float32)
    full = pltpu.VMEM((256, 256), jnp.float32)
    parts = pltpu.VMEM((n, wide, 256), jnp.float32)
    vmem = pl.BlockSpec(memory_space=pltpu.VMEM)
    hbm = pl.BlockSpec(memory_space=pltpu.HBM)
    arguments = (
        source_coords, source_weights, focus_steps, pupil_taps, blur_x, blur_y, blur_z
    )
    return pl.pallas_call(
        lambda *refs: plane_kernel(n, wide, *refs),
        out_shape=(square, square),
        in_specs=[hbm] * 8,
        out_specs=(vmem, vmem),
        scratch_shapes=[pltpu.VMEM((256, 256), jnp.int32)]
        + [pltpu.SMEM(value.shape, value.dtype) for value in arguments]
        + [pltpu.SemaphoreType.DMA((8,)), pltpu.VMEM((8, lanes), jnp.float32)]
        + [pltpu.VMEM((24, 128), jnp.float32)] * 4
        + [
            pltpu.VMEM((4, 512, 256), jnp.bfloat16),
            pltpu.VMEM((shifts, 256, 512), jnp.bfloat16),
            pltpu.VMEM((shifts, 512, 512), jnp.bfloat16),
            full,
            full,
            full,
            pltpu.VMEM((1, 128), jnp.int32),
            pltpu.VMEM((n, 1, 128), jnp.int32),
            pltpu.SMEM((n, 1, 128), jnp.int32),
            parts,
            parts,
            parts,
            parts,
            pltpu.SemaphoreType.DMA((3, n)),
            pltpu.SemaphoreType.DMA((3, n)),
            pltpu.SemaphoreType.DMA,
        ],
        compiler_params=pltpu.CompilerParams(
            vmem_limit_bytes=64 * 2**20 - 2**17, collective_id=0, has_side_effects=True
        ),
    )(layout_mask, *arguments)


def solution(mesh):
    in_specs = (P("groups", None), P("src", None), P("src"), P(), P(), P(), P(), P())
    out_specs = (P(("groups", "src"), None), P(("groups", "src"), None))
    body = plane_per_device if mesh.shape["src"] == 16 else on_device
    return jax.shard_map(
        body, mesh=mesh, in_specs=in_specs, out_specs=out_specs, check_vma=False
    )
```

```python
import math

import jax
import jax.numpy as jnp
from jax import lax
from jax.experimental import pallas as pl
from jax.experimental.pallas import tpu as pltpu
from jax.sharding import PartitionSpec as P

two_pi = 2.0 * math.pi
defocus_scale = 0.8
dose_scale = 2.0


def extended_2(block, sides, width):
    for axis, dim in sides:
        count = lax.axis_size(axis)
        forward = [(i, i + 1) for i in range(count - 1)]
        backward = [(target, source) for source, target in forward]
        low = lax.ppermute(
            lax.slice_in_dim(block, block.shape[dim] - width, None, axis=dim), axis, forward
        )
        high = lax.ppermute(lax.slice_in_dim(block, 0, width, axis=dim), axis, backward)
        block = jnp.concatenate([low, block, high], axis=dim)
    return block


def passed_along(block, axis, distance):
    devices = range(lax.axis_size(axis))
    route = [(i - distance, i) for i in devices if i - distance in devices]
    return lax.ppermute(block, axis, route)


def tap_matrix(out_pos, extent, tilt_index, focus_step, pupil_taps):
    tap_count = pupil_taps.shape[0]
    centre = (tap_count - 1) / 2.0
    column_pos = jnp.arange(extent, dtype=jnp.int32)
    offset = column_pos[None, :] - out_pos[:, None] + tap_count // 2
    inside = (offset >= 0) & (offset < tap_count)
    clipped = jnp.clip(offset, 0, tap_count - 1)
    amplitude = jnp.take(pupil_taps, clipped) / math.sqrt(tap_count)
    relative = clipped.astype(jnp.float32) - centre
    phase_angle = (
        two_pi * tilt_index.astype(jnp.float32) * relative / tap_count
        + defocus_scale * focus_step.astype(jnp.float32) * (relative / centre) ** 2
    )
    real_part = jnp.where(inside, amplitude * jnp.cos(phase_angle), jnp.zeros_like(amplitude))
    imag_part = jnp.where(inside, amplitude * jnp.sin(phase_angle), jnp.zeros_like(amplitude))
    return (real_part.astype(jnp.bfloat16), imag_part.astype(jnp.bfloat16))


def field_power(mask_bf, row_pos, tilt_x, tilt_y, focus_step, pupil_taps):
    rows_tile, cols_tile = mask_bf.shape
    row_count = row_pos.shape[0]
    col_pos = jnp.arange(cols_tile, dtype=jnp.int32)
    rows_real, rows_imag = tap_matrix(row_pos, rows_tile, tilt_y, focus_step, pupil_taps)
    cols_real, cols_imag = tap_matrix(col_pos, cols_tile, tilt_x, focus_step, pupil_taps)
    stacked = jnp.concatenate([rows_real, rows_imag], axis=0)
    first_pass = jnp.dot(stacked, mask_bf, preferred_element_type=jnp.float32).astype(jnp.bfloat16)
    joined = jnp.concatenate([first_pass[:row_count], first_pass[row_count:]], axis=1)
    upper_half = jnp.concatenate([cols_real.T, cols_imag.T], axis=1)
    lower_half = jnp.concatenate([-cols_imag.T, cols_real.T], axis=1)
    pupil_cols = jnp.concatenate([upper_half, lower_half], axis=0)
    field_parts = jnp.dot(joined, pupil_cols, preferred_element_type=jnp.float32)
    return field_parts[:, :cols_tile] ** 2 + field_parts[:, cols_tile:] ** 2


def on_device(
    layout_mask, source_coords, source_weights, focus_steps, pupil_taps, blur_x, blur_y, blur_z
):
    rows_tile, cols_tile = layout_mask.shape
    planes = focus_steps.shape[0]
    devices = lax.axis_size("src")
    src_local = source_coords.shape[0]
    mask_bf = layout_mask.astype(jnp.bfloat16)
    own_rows = planes * rows_tile // devices
    per_plane = devices // planes
    factors = source_weights.astype(jnp.float32) / (4.0 * src_local * devices)
    row_pos = jnp.arange(rows_tile, dtype=jnp.int32)

    def plane_term(focus_step):
        running = jnp.zeros((rows_tile, cols_tile), jnp.float32)
        for source in range(src_local):
            power = field_power(
                mask_bf,
                row_pos,
                source_coords[source, 0],
                source_coords[source, 1],
                focus_step,
                pupil_taps,
            )
            running = running + factors[source] * power
        return running

    partial_sum = lax.map(plane_term, focus_steps).reshape(planes * rows_tile, cols_tile)
    intensity = lax.psum_scatter(partial_sum, "src", scatter_dimension=0, tiled=True)
    acid_level = 1.0 - jnp.exp(-dose_scale * intensity)
    width_x = blur_x.shape[0]
    half_x = width_x // 2
    padded = jnp.pad(acid_level, ((0, 0), (half_x, half_x)))
    along_x = jnp.zeros_like(acid_level)
    for tap_index in range(width_x):
        along_x = (
            along_x + blur_x[tap_index] / width_x * padded[:, tap_index : tap_index + cols_tile]
        )
    width_y = blur_y.shape[0]
    half_y = width_y // 2
    extended = extended_2(along_x, (("src", 0),), half_y)
    along_y = jnp.zeros_like(along_x)
    for tap_index in range(width_y):
        along_y = along_y + blur_y[tap_index] / width_y * extended[tap_index : tap_index + own_rows]
    latent = blur_z[planes - 1] / planes * along_y
    for plane_lag in range(1 - planes, planes):
        if plane_lag != 0:
            arrived = passed_along(along_y, "src", plane_lag * per_plane)
            latent = latent + blur_z[plane_lag + planes - 1] / planes * arrived
    return (intensity, latent)


max_shift = 8
shifts = 2 * max_shift + 1
lanes = 512


def exact_dot(left, right):
    def halves(value):
        high = value.astype(jnp.bfloat16)
        return high, (value - high.astype(jnp.float32)).astype(jnp.bfloat16)

    def product(a, b):
        return jnp.dot(a, b, preferred_element_type=jnp.float32)

    left_high, left_low = halves(left)
    right_high, right_low = halves(right)
    return (
        product(left_high, right_low) + product(left_low, right_high)
    ) + product(left_high, right_high)


def store_toeplitz(row, position, pieces, apart=128):
    base = pltpu.roll(jnp.broadcast_to(row, (16, 128)), 0, 1, stride=1, stride_axis=0)
    lane = lax.broadcasted_iota(jnp.int32, (16, 128), 1)
    zero = jnp.zeros((16, 128), jnp.float32)
    for j in range(8):
        first = 16 * j + position - 256
        turn, tile = first % 128, first // 128
        rolled = pltpu.roll(base, turn, 1) if turn else base
        wraps = turn > 65
        kept = jnp.where(lane >= turn, rolled, zero) if wraps else rolled
        wrapped = jnp.where(lane < turn, rolled, zero) if wraps else zero
        for block, start in ((j, tile), (j + 8, tile + 1)):
            for column in range(2):
                part = kept if column == start else wrapped if column == start + 1 else zero
                for ref, top, side, sign in pieces:
                    value = part if sign > 0 else -part
                    left = side + apart * column
                    ref[top + 16 * block : top + 16 * block + 16, left : left + 128] = (
                        value.astype(ref.dtype)
                    )


def store_taps(taps_ref, row, focus, flip, real_ref, imag_ref, tap_count):
    centre = (tap_count - 1) / 2.0
    amplitude = taps_ref[row : row + 1, :128] / math.sqrt(tap_count)
    shape = (24, 128)
    relative = (lax.broadcasted_iota(jnp.int32, shape, 1).astype(jnp.float32) - centre) * flip
    tilt = (lax.broadcasted_iota(jnp.int32, shape, 0) - max_shift).astype(jnp.float32)
    phase = (
        two_pi * tilt * relative / tap_count + defocus_scale * focus * (relative / centre) ** 2
    )
    real_ref[...] = amplitude * jnp.cos(phase)
    imag_ref[...] = amplitude * jnp.sin(phase)


def build_tables(tap_count, mask_ref, rows_ref, focus, tap_refs, stacked_slots, fields, pupils):
    forward_real, forward_imag, back_real, back_imag = tap_refs
    store_taps(rows_ref, 0, focus, 1.0, forward_real, forward_imag, tap_count)
    store_taps(rows_ref, 1, focus, -1.0, back_real, back_imag, tap_count)
    mask_bf = mask_ref[...].astype(jnp.float32).astype(jnp.bfloat16)

    def one_shift(shift, slot):
        stacked = stacked_slots.at[slot]
        row = pl.ds(shift, 1)
        store_toeplitz(forward_real[row, :], 232, ((stacked, 0, 0, 1),))
        store_toeplitz(forward_imag[row, :], 232, ((stacked, 256, 0, 1),))
        first = jnp.dot(stacked[...], mask_bf, preferred_element_type=jnp.float32)
        fields[shift, :, :256] = first[:256].astype(jnp.bfloat16)
        fields[shift, :, 256:] = first[256:].astype(jnp.bfloat16)
        pupil = pupils.at[shift]
        store_toeplitz(back_real[row, :], 233, ((pupil, 0, 0, 1), (pupil, 256, 128, 1)), 256)
        store_toeplitz(back_imag[row, :], 233, ((pupil, 0, 128, 1), (pupil, 256, 0, -1)), 256)

    def four_shifts(step, carry):
        for slot in range(4):
            one_shift(4 * step + slot, slot)
        return carry

    lax.fori_loop(0, shifts // 4, four_shifts, 0)
    one_shift(shifts - 1, 0)


def lane_row(count, value):
    lane = lax.broadcasted_iota(jnp.int32, (1, lanes), 1)
    row = jnp.zeros((1, lanes), jnp.float32)
    for t in range(count):
        row = jnp.where(lane == t, value(t), row)
    return row


def plane_kernel(
    n, wide, mask_hbm, coords_hbm, weights_hbm, focus_hbm, taps_hbm, blur_x_hbm, blur_y_hbm,
    blur_z_hbm, intensity_ref, latent_ref, mask_ref, coords_ref, weights_ref, focus_ref, taps_ref,
    blur_x_ref, blur_y_ref, blur_z_ref, arg_sems, rows, t0, t1, t2, t3, stacked, fields, pupils, blur,
    centre, mix, own, points, points_smem, along, columns, mixed, planes, send_sems, recv_sems,
    local_sem,
):
    me = lax.axis_index("src")
    group = lax.axis_index("groups")
    local = weights_ref.shape[0]
    tap_count, blur_count = taps_ref.shape[0], blur_x_ref.shape[0]
    barrier = pltpu.get_barrier_semaphore()

    def each(action):
        lax.fori_loop(1, n, lambda off, carry: (action(off), carry)[1], 0)

    def peer(off):
        return (group, lax.rem(me + off, n))

    def signal(off):
        pl.semaphore_signal(
            barrier, inc=1, device_id=peer(off), device_id_type=pl.DeviceIdType.MESH
        )

    def copy(phase, source, target, off, slot):
        return pltpu.make_async_remote_copy(
            src_ref=source(off),
            dst_ref=target.at[slot],
            send_sem=send_sems.at[phase, off],
            recv_sem=recv_sems.at[phase, off],
            device_id=peer(off),
            device_id_type=pl.DeviceIdType.MESH,
        )

    def block_of(device):
        return device // 2 + lax.rem(device, 2) * (n // 2)

    def itself(device):
        return device

    def start(phase, source, target, place=itself, wanted=None):
        def one(off):
            transfer = copy(phase, source, target, off, place(me))
            if wanted is None:
                transfer.start()
            else:
                pl.when(wanted(block_of(lax.rem(me + off, n))))(transfer.start)

        each(one)

    def receive(phase, source, target, place=itself):
        each(
            lambda off: copy(
                phase, source, target, off, place(lax.rem(me + n - off, n))
            ).wait_recv()
        )

    def sent(phase, source, target, place=itself):
        each(lambda off: copy(phase, source, target, off, place(me)).wait_send())

    fetches = [
        pltpu.make_async_copy(source, target, arg_sems.at[place])
        for place, (source, target) in enumerate(
            (
                (coords_hbm, coords_ref),
                (weights_hbm, weights_ref),
                (focus_hbm, focus_ref),
                (taps_hbm, taps_ref),
                (blur_x_hbm, blur_x_ref),
                (blur_y_hbm, blur_y_ref),
                (blur_z_hbm, blur_z_ref),
                (mask_hbm, mask_ref),
            )
        )
    ]
    for fetch in fetches:
        fetch.start()
    each(signal)
    for fetch in fetches:
        fetch.wait()
    lane = lax.broadcasted_iota(jnp.int32, (1, 128), 1)
    packed = jnp.zeros((1, 128), jnp.int32)
    for s in range(local):
        packed = jnp.where(lane == 3 * s, coords_ref[s, 0], packed)
        packed = jnp.where(lane == 3 * s + 1, coords_ref[s, 1], packed)
        packed = jnp.where(lane == 3 * s + 2, weights_ref[s], packed)
    own[...] = packed
    points[me] = packed
    rows[0:1, :] = lane_row(tap_count, lambda t: taps_ref[t])
    rows[1:2, :] = lane_row(tap_count, lambda t: taps_ref[tap_count - 1 - t])
    rows[2:3, :] = lane_row(blur_count, lambda t: blur_x_ref[t] / blur_count)
    rows[3:4, :] = lane_row(blur_count, lambda t: blur_y_ref[blur_count - 1 - t] / blur_count)
    pl.semaphore_wait(barrier, n - 1)
    point_source = lambda off: own
    start(0, point_source, points)

    focus = focus_ref[me].astype(jnp.float32)
    build_tables(tap_count, mask_ref, rows, focus, (t0, t1, t2, t3), stacked, fields, pupils)
    store_toeplitz(rows[2:3, :128], 241, ((blur, 0, 0, 1),))
    intensity_ref[...] = jnp.zeros_like(intensity_ref)
    receive(0, point_source, points)
    to_smem = pltpu.make_async_copy(points, points_smem, local_sem)
    to_smem.start()
    to_smem.wait()

    def image_half(half):
        def four_devices(step, carry):
            power = jnp.zeros((256, 128), jnp.float32)
            for place in range(4 * local):
                device, s = 4 * step + place // local, place % local
                point = [points_smem[device, 0, 3 * s + item] for item in range(3)]
                factor = point[2].astype(jnp.float32) / (4.0 * local * n)
                field = jnp.dot(
                    fields[point[1] + max_shift],
                    pupils[point[0] + max_shift, :, 256 * half : 256 * half + 256],
                    preferred_element_type=jnp.float32,
                )
                power = power + factor * (field[:, :128] ** 2 + field[:, 128:] ** 2)
            intensity_ref[:, 128 * half : 128 * half + 128] += power
            return carry

        lax.fori_loop(0, n // 4, four_devices, 0)

    def acid_columns(stop):
        return (1.0 - jnp.exp(-dose_scale * intensity_ref[:, :stop])).T

    early = (128 - blur_count // 2) // wide
    column_source = lambda off: along.at[block_of(lax.rem(me + off, n))]
    image_half(0)
    along[:early] = exact_dot(blur[: early * wide, :128], acid_columns(128)).reshape(
        early, wide, 256
    )
    start(1, column_source, columns, wanted=lambda block: block < early)
    image_half(1)
    along[early:] = exact_dot(blur[early * wide :, :], acid_columns(256)).reshape(
        n - early, wide, 256
    )
    start(1, column_source, columns, wanted=lambda block: block >= early)
    columns[me] = along[block_of(me)]

    back_y = rows[3:4, :]
    store_toeplitz(rows[3:4, :128], 241, ((centre, 0, 0, 1),))
    tall = jnp.broadcast_to(back_y, (16, lanes))
    before = pltpu.roll(tall, lanes - 31, 1, stride=1, stride_axis=0)[:, :256]
    after = pltpu.roll(tall, 241, 1, stride=1, stride_axis=0)[:, :256]
    pad = jnp.zeros((112, 256), jnp.float32)
    distance = lax.broadcasted_iota(jnp.int32, (256, 256), 0) - lax.broadcasted_iota(
        jnp.int32, (256, 256), 1
    )
    mix[...] = jnp.zeros_like(mix)
    for lag in range(1 - n, n):
        mix[...] = jnp.where(distance == lag * wide, blur_z_ref[lag + n - 1] / n, mix[...])

    receive(1, column_source, columns)
    stack = columns[...].reshape(256, 256)
    zero = jnp.zeros((wide, 128), jnp.float32)
    along_y = (
        exact_dot(stack, centre[...])
        + exact_dot(
            jnp.concatenate([zero, stack[:-wide, 128:]], axis=0),
            jnp.concatenate([pad, before], axis=0),
        )
        + exact_dot(
            jnp.concatenate([stack[wide:, :128], zero], axis=0),
            jnp.concatenate([after, pad], axis=0),
        )
    )
    mixed[...] = exact_dot(mix[...], along_y).reshape(n, wide, 256)
    plane_source = lambda off: mixed.at[lax.rem(me + off, n)]
    start(2, plane_source, planes, block_of)
    planes[block_of(me)] = mixed[me]
    sent(0, point_source, points)
    sent(1, column_source, columns)
    receive(2, plane_source, planes, block_of)
    latent_ref[...] = planes[...].reshape(256, 256).T
    sent(2, plane_source, planes, block_of)


def plane_per_device(
    layout_mask, source_coords, source_weights, focus_steps, pupil_taps, blur_x, blur_y, blur_z
):
    n = lax.axis_size("src")
    wide = layout_mask.shape[1] // n
    square = jax.ShapeDtypeStruct((256, 256), jnp.float32)
    full = pltpu.VMEM((256, 256), jnp.float32)
    parts = pltpu.VMEM((n, wide, 256), jnp.float32)
    vmem = pl.BlockSpec(memory_space=pltpu.VMEM)
    hbm = pl.BlockSpec(memory_space=pltpu.HBM)
    arguments = (
        source_coords, source_weights, focus_steps, pupil_taps, blur_x, blur_y, blur_z
    )
    return pl.pallas_call(
        lambda *refs: plane_kernel(n, wide, *refs),
        out_shape=(square, square),
        in_specs=[hbm] * 8,
        out_specs=(vmem, vmem),
        scratch_shapes=[pltpu.VMEM((256, 256), jnp.int32)]
        + [pltpu.SMEM(value.shape, value.dtype) for value in arguments]
        + [pltpu.SemaphoreType.DMA((8,)), pltpu.VMEM((8, lanes), jnp.float32)]
        + [pltpu.VMEM((24, 128), jnp.float32)] * 4
        + [
            pltpu.VMEM((4, 512, 256), jnp.bfloat16),
            pltpu.VMEM((shifts, 256, 512), jnp.bfloat16),
            pltpu.VMEM((shifts, 512, 512), jnp.bfloat16),
            full,
            full,
            full,
            pltpu.VMEM((1, 128), jnp.int32),
            pltpu.VMEM((n, 1, 128), jnp.int32),
            pltpu.SMEM((n, 1, 128), jnp.int32),
            parts,
            parts,
            parts,
            parts,
            pltpu.SemaphoreType.DMA((3, n)),
            pltpu.SemaphoreType.DMA((3, n)),
            pltpu.SemaphoreType.DMA,
        ],
        compiler_params=pltpu.CompilerParams(
            vmem_limit_bytes=64 * 2**20 - 2**17, collective_id=0, has_side_effects=True
        ),
    )(layout_mask, *arguments)


def solution(mesh):
    in_specs = (P("groups", None), P("src", None), P("src"), P(), P(), P(), P(), P())
    out_specs = (P(("groups", "src"), None), P(("groups", "src"), None))
    body = plane_per_device if mesh.shape["src"] == 16 else on_device
    return jax.shard_map(
        body, mesh=mesh, in_specs=in_specs, out_specs=out_specs, check_vma=False
    )
```

```python
import math

import jax
import jax.numpy as jnp
from jax import lax
from jax.experimental import pallas as pl
from jax.experimental.pallas import tpu as pltpu
from jax.sharding import PartitionSpec as P

two_pi = 2.0 * math.pi
defocus_scale = 0.8
dose_scale = 2.0


def extended_2(block, sides, width):
    for axis, dim in sides:
        count = lax.axis_size(axis)
        forward = [(i, i + 1) for i in range(count - 1)]
        backward = [(target, source) for source, target in forward]
        low = lax.ppermute(
            lax.slice_in_dim(block, block.shape[dim] - width, None, axis=dim), axis, forward
        )
        high = lax.ppermute(lax.slice_in_dim(block, 0, width, axis=dim), axis, backward)
        block = jnp.concatenate([low, block, high], axis=dim)
    return block


def passed_along(block, axis, distance):
    devices = range(lax.axis_size(axis))
    route = [(i - distance, i) for i in devices if i - distance in devices]
    return lax.ppermute(block, axis, route)


def tap_matrix(out_pos, extent, tilt_index, focus_step, pupil_taps):
    tap_count = pupil_taps.shape[0]
    centre = (tap_count - 1) / 2.0
    column_pos = jnp.arange(extent, dtype=jnp.int32)
    offset = column_pos[None, :] - out_pos[:, None] + tap_count // 2
    inside = (offset >= 0) & (offset < tap_count)
    clipped = jnp.clip(offset, 0, tap_count - 1)
    amplitude = jnp.take(pupil_taps, clipped) / math.sqrt(tap_count)
    relative = clipped.astype(jnp.float32) - centre
    phase_angle = (
        two_pi * tilt_index.astype(jnp.float32) * relative / tap_count
        + defocus_scale * focus_step.astype(jnp.float32) * (relative / centre) ** 2
    )
    real_part = jnp.where(inside, amplitude * jnp.cos(phase_angle), jnp.zeros_like(amplitude))
    imag_part = jnp.where(inside, amplitude * jnp.sin(phase_angle), jnp.zeros_like(amplitude))
    return (real_part.astype(jnp.bfloat16), imag_part.astype(jnp.bfloat16))


def field_power(mask_bf, row_pos, tilt_x, tilt_y, focus_step, pupil_taps):
    rows_tile, cols_tile = mask_bf.shape
    row_count = row_pos.shape[0]
    col_pos = jnp.arange(cols_tile, dtype=jnp.int32)
    rows_real, rows_imag = tap_matrix(row_pos, rows_tile, tilt_y, focus_step, pupil_taps)
    cols_real, cols_imag = tap_matrix(col_pos, cols_tile, tilt_x, focus_step, pupil_taps)
    stacked = jnp.concatenate([rows_real, rows_imag], axis=0)
    first_pass = jnp.dot(stacked, mask_bf, preferred_element_type=jnp.float32).astype(jnp.bfloat16)
    joined = jnp.concatenate([first_pass[:row_count], first_pass[row_count:]], axis=1)
    upper_half = jnp.concatenate([cols_real.T, cols_imag.T], axis=1)
    lower_half = jnp.concatenate([-cols_imag.T, cols_real.T], axis=1)
    pupil_cols = jnp.concatenate([upper_half, lower_half], axis=0)
    field_parts = jnp.dot(joined, pupil_cols, preferred_element_type=jnp.float32)
    return field_parts[:, :cols_tile] ** 2 + field_parts[:, cols_tile:] ** 2


def on_device(
    layout_mask, source_coords, source_weights, focus_steps, pupil_taps, blur_x, blur_y, blur_z
):
    rows_tile, cols_tile = layout_mask.shape
    planes = focus_steps.shape[0]
    devices = lax.axis_size("src")
    src_local = source_coords.shape[0]
    mask_bf = layout_mask.astype(jnp.bfloat16)
    own_rows = planes * rows_tile // devices
    per_plane = devices // planes
    factors = source_weights.astype(jnp.float32) / (4.0 * src_local * devices)
    row_pos = jnp.arange(rows_tile, dtype=jnp.int32)

    def plane_term(focus_step):
        running = jnp.zeros((rows_tile, cols_tile), jnp.float32)
        for source in range(src_local):
            power = field_power(
                mask_bf,
                row_pos,
                source_coords[source, 0],
                source_coords[source, 1],
                focus_step,
                pupil_taps,
            )
            running = running + factors[source] * power
        return running

    partial_sum = lax.map(plane_term, focus_steps).reshape(planes * rows_tile, cols_tile)
    intensity = lax.psum_scatter(partial_sum, "src", scatter_dimension=0, tiled=True)
    acid_level = 1.0 - jnp.exp(-dose_scale * intensity)
    width_x = blur_x.shape[0]
    half_x = width_x // 2
    padded = jnp.pad(acid_level, ((0, 0), (half_x, half_x)))
    along_x = jnp.zeros_like(acid_level)
    for tap_index in range(width_x):
        along_x = (
            along_x + blur_x[tap_index] / width_x * padded[:, tap_index : tap_index + cols_tile]
        )
    width_y = blur_y.shape[0]
    half_y = width_y // 2
    extended = extended_2(along_x, (("src", 0),), half_y)
    along_y = jnp.zeros_like(along_x)
    for tap_index in range(width_y):
        along_y = along_y + blur_y[tap_index] / width_y * extended[tap_index : tap_index + own_rows]
    latent = blur_z[planes - 1] / planes * along_y
    for plane_lag in range(1 - planes, planes):
        if plane_lag != 0:
            arrived = passed_along(along_y, "src", plane_lag * per_plane)
            latent = latent + blur_z[plane_lag + planes - 1] / planes * arrived
    return (intensity, latent)


max_shift = 8
shifts = 2 * max_shift + 1
lanes = 512


def exact_dot(left, right):
    def halves(value):
        high = value.astype(jnp.bfloat16)
        return high, (value - high.astype(jnp.float32)).astype(jnp.bfloat16)

    def product(a, b):
        return jnp.dot(a, b, preferred_element_type=jnp.float32)

    left_high, left_low = halves(left)
    right_high, right_low = halves(right)
    return (
        product(left_high, right_low) + product(left_low, right_high)
    ) + product(left_high, right_high)


def store_toeplitz(row, position, pieces, apart=128):
    base = pltpu.roll(jnp.broadcast_to(row, (16, 128)), 0, 1, stride=1, stride_axis=0)
    lane = lax.broadcasted_iota(jnp.int32, (16, 128), 1)
    zero = jnp.zeros((16, 128), jnp.float32)
    for j in range(8):
        first = 16 * j + position - 256
        turn, tile = first % 128, first // 128
        rolled = pltpu.roll(base, turn, 1) if turn else base
        wraps = turn > 65
        kept = jnp.where(lane >= turn, rolled, zero) if wraps else rolled
        wrapped = jnp.where(lane < turn, rolled, zero) if wraps else zero
        for block, start in ((j, tile), (j + 8, tile + 1)):
            for column in range(2):
                part = kept if column == start else wrapped if column == start + 1 else zero
                for ref, top, side, sign in pieces:
                    value = part if sign > 0 else -part
                    left = side + apart * column
                    ref[top + 16 * block : top + 16 * block + 16, left : left + 128] = (
                        value.astype(ref.dtype)
                    )


def store_taps(taps_ref, row, focus, flip, real_ref, imag_ref, tap_count):
    centre = (tap_count - 1) / 2.0
    amplitude = taps_ref[row : row + 1, :128] / math.sqrt(tap_count)
    shape = (24, 128)
    relative = (lax.broadcasted_iota(jnp.int32, shape, 1).astype(jnp.float32) - centre) * flip
    tilt = (lax.broadcasted_iota(jnp.int32, shape, 0) - max_shift).astype(jnp.float32)
    phase = (
        two_pi * tilt * relative / tap_count + defocus_scale * focus * (relative / centre) ** 2
    )
    real_ref[...] = amplitude * jnp.cos(phase)
    imag_ref[...] = amplitude * jnp.sin(phase)


def build_tables(tap_count, mask_ref, rows_ref, focus, tap_refs, stacked_slots, fields, pupils):
    forward_real, forward_imag, back_real, back_imag = tap_refs
    store_taps(rows_ref, 0, focus, 1.0, forward_real, forward_imag, tap_count)
    store_taps(rows_ref, 1, focus, -1.0, back_real, back_imag, tap_count)
    mask_bf = mask_ref[...].astype(jnp.float32).astype(jnp.bfloat16)

    def one_shift(shift, slot):
        stacked = stacked_slots.at[slot]
        row = pl.ds(shift, 1)
        store_toeplitz(forward_real[row, :], 232, ((stacked, 0, 0, 1),))
        store_toeplitz(forward_imag[row, :], 232, ((stacked, 256, 0, 1),))
        first = jnp.dot(stacked[...], mask_bf, preferred_element_type=jnp.float32)
        fields[shift, :, :256] = first[:256].astype(jnp.bfloat16)
        fields[shift, :, 256:] = first[256:].astype(jnp.bfloat16)
        pupil = pupils.at[shift]
        store_toeplitz(back_real[row, :], 233, ((pupil, 0, 0, 1), (pupil, 256, 128, 1)), 256)
        store_toeplitz(back_imag[row, :], 233, ((pupil, 0, 128, 1), (pupil, 256, 0, -1)), 256)

    def four_shifts(step, carry):
        for slot in range(4):
            one_shift(4 * step + slot, slot)
        return carry

    lax.fori_loop(0, shifts // 4, four_shifts, 0)
    one_shift(shifts - 1, 0)


def lane_row(count, value):
    lane = lax.broadcasted_iota(jnp.int32, (1, lanes), 1)
    row = jnp.zeros((1, lanes), jnp.float32)
    for t in range(count):
        row = jnp.where(lane == t, value(t), row)
    return row


def plane_kernel(
    n, wide, mask_hbm, coords_hbm, weights_hbm, focus_hbm, taps_hbm, blur_x_hbm, blur_y_hbm,
    blur_z_hbm, intensity_ref, latent_ref, mask_ref, coords_ref, weights_ref, focus_ref, taps_ref,
    blur_x_ref, blur_y_ref, blur_z_ref, arg_sems, rows, t0, t1, t2, t3, stacked, fields, pupils, blur,
    centre, mix, own, points, points_smem, along, columns, mixed, planes, send_sems, recv_sems,
    local_sem,
):
    me = lax.axis_index("src")
    group = lax.axis_index("groups")
    local = weights_ref.shape[0]
    tap_count, blur_count = taps_ref.shape[0], blur_x_ref.shape[0]
    barrier = pltpu.get_barrier_semaphore()

    def each(action):
        lax.fori_loop(1, n, lambda off, carry: (action(off), carry)[1], 0)

    def peer(off):
        return (group, lax.rem(me + off, n))

    def signal(off):
        pl.semaphore_signal(
            barrier, inc=1, device_id=peer(off), device_id_type=pl.DeviceIdType.MESH
        )

    def copy(phase, source, target, off, slot):
        return pltpu.make_async_remote_copy(
            src_ref=source(off),
            dst_ref=target.at[slot],
            send_sem=send_sems.at[phase, off],
            recv_sem=recv_sems.at[phase, off],
            device_id=peer(off),
            device_id_type=pl.DeviceIdType.MESH,
        )

    def block_of(device):
        return device // 2 + lax.rem(device, 2) * (n // 2)

    def itself(device):
        return device

    def start(phase, source, target, place=itself, wanted=None):
        def one(turn):
            off = lax.rem(turn + n // 2 - 2, n - 1) + 1
            transfer = copy(phase, source, target, off, place(me))
            if wanted is None:
                transfer.start()
            else:
                pl.when(wanted(block_of(lax.rem(me + off, n))))(transfer.start)

        each(one)

    def receive(phase, source, target, place=itself):
        each(
            lambda off: copy(
                phase, source, target, off, place(lax.rem(me + n - off, n))
            ).wait_recv()
        )

    def sent(phase, source, target, place=itself):
        each(lambda off: copy(phase, source, target, off, place(me)).wait_send())

    fetches = [
        pltpu.make_async_copy(source, target, arg_sems.at[place])
        for place, (source, target) in enumerate(
            (
                (coords_hbm, coords_ref),
                (weights_hbm, weights_ref),
                (focus_hbm, focus_ref),
                (taps_hbm, taps_ref),
                (blur_x_hbm, blur_x_ref),
                (blur_y_hbm, blur_y_ref),
                (blur_z_hbm, blur_z_ref),
                (mask_hbm, mask_ref),
            )
        )
    ]
    for fetch in fetches:
        fetch.start()
    each(signal)
    for fetch in fetches:
        fetch.wait()
    lane = lax.broadcasted_iota(jnp.int32, (1, 128), 1)
    packed = jnp.zeros((1, 128), jnp.int32)
    for s in range(local):
        packed = jnp.where(lane == 3 * s, coords_ref[s, 0], packed)
        packed = jnp.where(lane == 3 * s + 1, coords_ref[s, 1], packed)
        packed = jnp.where(lane == 3 * s + 2, weights_ref[s], packed)
    own[...] = packed
    points[me] = packed
    rows[0:1, :] = lane_row(tap_count, lambda t: taps_ref[t])
    rows[1:2, :] = lane_row(tap_count, lambda t: taps_ref[tap_count - 1 - t])
    rows[2:3, :] = lane_row(blur_count, lambda t: blur_x_ref[t] / blur_count)
    rows[3:4, :] = lane_row(blur_count, lambda t: blur_y_ref[blur_count - 1 - t] / blur_count)
    pl.semaphore_wait(barrier, n - 1)
    point_source = lambda off: own
    start(0, point_source, points)

    focus = focus_ref[me].astype(jnp.float32)
    build_tables(tap_count, mask_ref, rows, focus, (t0, t1, t2, t3), stacked, fields, pupils)
    store_toeplitz(rows[2:3, :128], 241, ((blur, 0, 0, 1),))
    intensity_ref[...] = jnp.zeros_like(intensity_ref)
    receive(0, point_source, points)
    to_smem = pltpu.make_async_copy(points, points_smem, local_sem)
    to_smem.start()
    to_smem.wait()

    def image_half(half):
        def four_devices(step, carry):
            power = jnp.zeros((256, 128), jnp.float32)
            for place in range(4 * local):
                device, s = 4 * step + place // local, place % local
                point = [points_smem[device, 0, 3 * s + item] for item in range(3)]
                factor = point[2].astype(jnp.float32) / (4.0 * local * n)
                field = jnp.dot(
                    fields[point[1] + max_shift],
                    pupils[point[0] + max_shift, :, 256 * half : 256 * half + 256],
                    preferred_element_type=jnp.float32,
                )
                power = power + factor * (field[:, :128] ** 2 + field[:, 128:] ** 2)
            intensity_ref[:, 128 * half : 128 * half + 128] += power
            return carry

        lax.fori_loop(0, n // 4, four_devices, 0)

    def acid_columns(stop):
        return (1.0 - jnp.exp(-dose_scale * intensity_ref[:, :stop])).T

    early = (128 - blur_count // 2) // wide
    column_source = lambda off: along.at[block_of(lax.rem(me + off, n))]
    image_half(0)
    along[:early] = exact_dot(blur[: early * wide, :128], acid_columns(128)).reshape(
        early, wide, 256
    )
    start(1, column_source, columns, wanted=lambda block: block < early)
    image_half(1)
    along[early:] = exact_dot(blur[early * wide :, :], acid_columns(256)).reshape(
        n - early, wide, 256
    )
    start(1, column_source, columns, wanted=lambda block: block >= early)
    columns[me] = along[block_of(me)]

    back_y = rows[3:4, :]
    store_toeplitz(rows[3:4, :128], 241, ((centre, 0, 0, 1),))
    tall = jnp.broadcast_to(back_y, (16, lanes))
    before = pltpu.roll(tall, lanes - 31, 1, stride=1, stride_axis=0)[:, :256]
    after = pltpu.roll(tall, 241, 1, stride=1, stride_axis=0)[:, :256]
    pad = jnp.zeros((112, 256), jnp.float32)
    distance = lax.broadcasted_iota(jnp.int32, (256, 256), 0) - lax.broadcasted_iota(
        jnp.int32, (256, 256), 1
    )
    mix[...] = jnp.zeros_like(mix)
    for lag in range(1 - n, n):
        mix[...] = jnp.where(distance == lag * wide, blur_z_ref[lag + n - 1] / n, mix[...])

    receive(1, column_source, columns)
    stack = columns[...].reshape(256, 256)
    zero = jnp.zeros((wide, 128), jnp.float32)
    along_y = (
        exact_dot(stack, centre[...])
        + exact_dot(
            jnp.concatenate([zero, stack[:-wide, 128:]], axis=0),
            jnp.concatenate([pad, before], axis=0),
        )
        + exact_dot(
            jnp.concatenate([stack[wide:, :128], zero], axis=0),
            jnp.concatenate([after, pad], axis=0),
        )
    )
    mixed[...] = exact_dot(mix[...], along_y).reshape(n, wide, 256)
    plane_source = lambda off: mixed.at[lax.rem(me + off, n)]
    start(2, plane_source, planes, block_of)
    planes[block_of(me)] = mixed[me]
    sent(0, point_source, points)
    sent(1, column_source, columns)
    receive(2, plane_source, planes, block_of)
    latent_ref[...] = planes[...].reshape(256, 256).T
    sent(2, plane_source, planes, block_of)


def plane_per_device(
    layout_mask, source_coords, source_weights, focus_steps, pupil_taps, blur_x, blur_y, blur_z
):
    n = lax.axis_size("src")
    wide = layout_mask.shape[1] // n
    square = jax.ShapeDtypeStruct((256, 256), jnp.float32)
    full = pltpu.VMEM((256, 256), jnp.float32)
    parts = pltpu.VMEM((n, wide, 256), jnp.float32)
    vmem = pl.BlockSpec(memory_space=pltpu.VMEM)
    hbm = pl.BlockSpec(memory_space=pltpu.HBM)
    arguments = (
        source_coords, source_weights, focus_steps, pupil_taps, blur_x, blur_y, blur_z
    )
    return pl.pallas_call(
        lambda *refs: plane_kernel(n, wide, *refs),
        out_shape=(square, square),
        in_specs=[hbm] * 8,
        out_specs=(vmem, vmem),
        scratch_shapes=[pltpu.VMEM((256, 256), jnp.int32)]
        + [pltpu.SMEM(value.shape, value.dtype) for value in arguments]
        + [pltpu.SemaphoreType.DMA((8,)), pltpu.VMEM((8, lanes), jnp.float32)]
        + [pltpu.VMEM((24, 128), jnp.float32)] * 4
        + [
            pltpu.VMEM((4, 512, 256), jnp.bfloat16),
            pltpu.VMEM((shifts, 256, 512), jnp.bfloat16),
            pltpu.VMEM((shifts, 512, 512), jnp.bfloat16),
            full,
            full,
            full,
            pltpu.VMEM((1, 128), jnp.int32),
            pltpu.VMEM((n, 1, 128), jnp.int32),
            pltpu.SMEM((n, 1, 128), jnp.int32),
            parts,
            parts,
            parts,
            parts,
            pltpu.SemaphoreType.DMA((3, n)),
            pltpu.SemaphoreType.DMA((3, n)),
            pltpu.SemaphoreType.DMA,
        ],
        compiler_params=pltpu.CompilerParams(
            vmem_limit_bytes=64 * 2**20 - 2**17, collective_id=0, has_side_effects=True
        ),
    )(layout_mask, *arguments)


def solution(mesh):
    in_specs = (P("groups", None), P("src", None), P("src"), P(), P(), P(), P(), P())
    out_specs = (P(("groups", "src"), None), P(("groups", "src"), None))
    body = plane_per_device if mesh.shape["src"] == 16 else on_device
    return jax.shard_map(
        body, mesh=mesh, in_specs=in_specs, out_specs=out_specs, check_vma=False
    )
```
